32 devices in a mesh: fsdp: 4 (over x, core), seq: 8 (over z, y).
Axes of the slice: x: 2, y: 2, z: 4, core: 2. Of those that a mesh axis runs over, the one named last changes fastest.
Arguments:
- tiles: bfloat16 [4, 4096, 768], P('fsdp', 'seq'), may hold values from -6 to 6
- documents: int32 [4, 4096], P('fsdp', 'seq'), may hold values from 0 to 3, never falling along the last dimension, each value on 1 to 2048 neighbouring positions
- cotangent: bfloat16 [4, 4096, 768], P('fsdp', 'seq'), may hold values from -6 to 6
- w_qkv: bfloat16 [768, 2304], P('fsdp'), may hold values from -0.21875 to 0.21875
- w_out: bfloat16 [768, 768], P('fsdp'), may hold values from -4 to 4
- w_up: bfloat16 [768, 3072], P('fsdp'), may hold values from -0.21875 to 0.21875
- w_down: bfloat16 [3072, 768], P('fsdp'), may hold values from -0.109375 to 0.109375
- gains: bfloat16 [2, 768], P(None, 'fsdp'), may hold values from 0.5 to 1.5
- shifts: bfloat16 [6, 768], P(None, 'fsdp'), may hold values from -1.5 to 1.5
- hidden_bias: bfloat16 [3072], P('fsdp'), may hold values from -3 to 3
Outputs:
- encoded: bfloat16 [4, 4096, 768], P('fsdp', 'seq')
- grad_tiles: bfloat16 [4, 4096, 768], P('fsdp', 'seq')
- grad_qkv: float32 [768, 2304], P('fsdp')
- grad_out_proj: float32 [768, 768], P('fsdp')
- grad_up: float32 [768, 3072], P('fsdp')
- grad_down: float32 [3072, 768], P('fsdp')
- grad_gains: float32 [2, 768], P(None, 'fsdp')
- grad_shifts: float32 [6, 768], P(None, 'fsdp')
- grad_hidden_bias: float32 [3072], P('fsdp')
The draws below stay inside these ranges and needn't reach their ends.
Inputs may be any that keep to these rules, and one draw needn't show every extreme that they name: `documents`: 4 slides packed in each sequence: ids never fall along a sequence, each slide has at least one token and at most half of the sequence's tokens, and one slide of each sequence has exactly half of them.
All inputs are finite; a program needn't handle non-finite values.
Results may differ from the reference program's by a relative error of at most 0.014.
Values may be sent and summed in bfloat16 or wider, within the bound.
No kernel may reach another device: no remote copies, remote signals or barrier semaphores. Data moves between devices by JAX's collectives and lax.ppermute only.
A program may use at most 320 MiB of HBM per device.

```python
import math
import jax
import jax.numpy as jnp
import numpy as np
from jax import lax

D = 768
HEADS = 16
FF = 3072
SEG_BASE = 1024
BRANCHES = 5
DOCS = 4
LENGTH = 4096
PACKS = 4


def draw_shifts(key, part):
    key = jax.random.fold_in(key, 17)
    row_scales = jnp.array([0.5, 0.5, 0.05, 0.05, 0.5, 0.5], jnp.float32)[:, None]
    values = jax.random.normal(key, (6, D), jnp.float32)
    return (jnp.clip(values, -3.0, 3.0) * row_scales).astype(jnp.bfloat16)


def shard_levels(rng, dims, cuts, least, high):
    gain, own = 1.0, jax.random.fold_in(rng, 6)
    for dim, parts in cuts:
        steps = jnp.exp(jax.random.uniform(jax.random.fold_in(own, dim), (parts,), jnp.float32, least / len(cuts), high / len(cuts)))
        gain = gain * jnp.repeat(steps, dims[dim] // parts).reshape([-1 if axis == dim else 1 for axis in range(len(dims))])
    return gain


def split_up(amount, total, most, lean):
    loads = [(1 << 20) // math.isqrt(grade ** lean) + 1 for grade in range(2, amount + 1)]
    surplus, holding = total - most - (amount - 1), [1] * (amount - 1)
    while surplus > 0:
        free = [i for i in range(amount - 1) if holding[i] < most]
        pool, remaining = sum([loads[i] for i in free]), surplus
        for i in free:
            more = min(most - holding[i], max(1, remaining * loads[i] // pool), surplus)
            holding[i] = holding[i] + more
            surplus = surplus - more
    return np.array([most] + holding)


def uneven_parts(own_key, amount, total, bound, slope):
    if amount == 2:
        one = jax.random.randint(own_key, (), max(1, total - bound), min(bound, total - 1) + 1)
        return jnp.stack([one, total - one])
    tallies = jnp.asarray(split_up(amount, total, bound, slope), jnp.int32)
    pairs = (amount - 1) // 2
    giver, taker = tallies[1:1 + 2 * pairs:2], tallies[2:2 + 2 * pairs:2]
    room = jnp.minimum(giver - 1, bound - taker)
    passed = jax.random.randint(jax.random.fold_in(own_key, 1), (pairs,), 0, 1 << 20) % (room + 1)
    tallies = tallies.at[1:1 + 2 * pairs:2].set(giver - passed).at[2:2 + 2 * pairs:2].set(taker + passed)
    return tallies[jax.random.permutation(jax.random.fold_in(own_key, 2), amount)]


def scatter_about(key, extent, width, bound, cuts=(), kind=jnp.bfloat16):
    values = width * jax.random.normal(key, extent, jnp.float32)
    if cuts:
        values = values * shard_levels(key, extent, cuts, -0.22, 0.18)
    return jnp.clip(values, -bound, bound).astype(kind)


def setup_inputs(seed: int = 0) -> dict:
    key_list = jax.random.split(jax.random.key(seed), 11)
    tiles = scatter_about(key_list[0], (PACKS, LENGTH, D), 1.0, 6.0, ((0, 4), (1, 8)))
    documents = jax.vmap(lambda own: jnp.searchsorted(jnp.cumsum(uneven_parts(own, DOCS, LENGTH, LENGTH // 2, 0)), jnp.arange(LENGTH), side="right"))(jax.random.split(key_list[1], PACKS)).reshape((PACKS, LENGTH)).astype(jnp.int32)
    cotangent = scatter_about(key_list[2], (PACKS, LENGTH, D), 1.0, 6.0, ((0, 4), (1, 8)))
    w_qkv = scatter_about(key_list[3], (D, 3 * D), D ** -0.5, 0.21875, ((0, 4),))
    w_out = scatter_about(key_list[4], (D, D), (max(D // 384, 1)) ** -0.5, 4.0, ((0, 4),))
    w_up = scatter_about(key_list[5], (D, FF), D ** -0.5, 0.21875, ((0, 4),))
    w_down = scatter_about(key_list[6], (FF, D), FF ** -0.5, 0.109375, ((0, 4),))
    gains = jnp.clip(1.0 + 0.1 * jax.random.normal(key_list[7], (2, D), jnp.float32), 0.5, 1.5).astype(jnp.bfloat16)
    shifts = draw_shifts(jax.random.fold_in(key_list[10], 71), 0)
    hidden_bias = scatter_about(key_list[9], (FF,), 0.5, 3.0, ((0, 4),))
    return dict(tiles=tiles, documents=documents, cotangent=cotangent, w_qkv=w_qkv, w_out=w_out, w_up=w_up, w_down=w_down, gains=gains, shifts=shifts, hidden_bias=hidden_bias)


@jax.custom_vjp
def low(v):
    return lax.optimization_barrier(v.astype(jnp.bfloat16)).astype(jnp.float32)

@jax.custom_vjp
def low_back(v):
    return v

def low_keep(v):
    return (low(v), None)

def low_pass(kept, grad):
    return (grad,)

def back_keep(v):
    return (v, None)

def back_low(kept, grad):
    return (low(grad),)
low.defvjp(low_keep, low_pass)
low_back.defvjp(back_keep, back_low)
highest = lax.Precision.HIGHEST
epsilon = 1e-05
masked = -1e+30

def layer_norm(values, gain_row, shift_row):
    center = lax.optimization_barrier(jnp.mean(values, axis=-1, keepdims=True))
    centered = values - center
    variance = lax.optimization_barrier(jnp.mean(centered * centered, axis=-1, keepdims=True))
    return centered * lax.rsqrt(variance + epsilon) * gain_row + shift_row

def picker(dilation, head_count):
    return jnp.arange(dilation)[:, None] == (jnp.arange(head_count) % dilation)[None, :]

def segment_attend(pieces):
    queries, key_rows, value_rows, query_docs, key_docs = pieces
    scaling = queries.shape[-1] ** (-0.5)
    scores = low_back(jnp.einsum('qhd,khd->hqk', queries, key_rows, precision=highest) * scaling)
    allowed = query_docs.T[:, :, None] == key_docs.T[:, None, :]
    scores = jnp.where(allowed, scores, masked)
    summit = lax.optimization_barrier(jnp.max(scores, axis=-1, keepdims=True))
    log_total = summit[..., 0] + jnp.log(lax.optimization_barrier(jnp.sum(jnp.exp(scores - summit), axis=-1)))
    weights = jnp.exp(scores - log_total[..., None])
    output = low_back(jnp.einsum('hqk,khd->qhd', low(weights), value_rows, precision=highest))
    return (output, log_total.T)

def branch_attend(queries, key_rows, value_rows, doc_ids, dilation, segment):
    length, head_count, head_dim = queries.shape
    pick_bool = picker(dilation, head_count)
    pick_float = pick_bool.astype(queries.dtype)
    pick_int = pick_bool.astype(jnp.int32)
    seg_count = length // segment
    row_count = segment // dilation

    def select(tensor):
        shaped = tensor.reshape(seg_count, row_count, dilation, head_count, head_dim)
        return lax.optimization_barrier(jnp.sum(shaped * pick_float[None, None, :, :, None], axis=2))
    doc_rows = lax.optimization_barrier(jnp.sum(doc_ids.reshape(seg_count, row_count, dilation, 1) * pick_int[None, None], axis=2))
    outputs, log_totals = lax.map(jax.checkpoint(segment_attend), (select(queries), select(key_rows), select(value_rows), doc_rows, doc_rows))
    spread_out = (outputs[:, :, None] * pick_float[None, None, :, :, None]).reshape(length, head_count, head_dim)
    log_full = jnp.where(pick_bool[None, None], log_totals[:, :, None, :], masked).reshape(length, head_count)
    return (spread_out, log_full)

def dilated_attention(queries, key_rows, value_rows, doc_ids):
    length = queries.shape[0]
    out_list = []
    log_list = []
    for branch in range(BRANCHES):
        dilation = 2 ** branch
        segment = min(SEG_BASE * dilation, length)
        branch_out, branch_log = branch_attend(queries, key_rows, value_rows, doc_ids, dilation, segment)
        out_list.append(branch_out)
        log_list.append(branch_log)
    log_stack = jnp.stack(log_list)
    summit = lax.optimization_barrier(jnp.max(log_stack, axis=0))
    log_all = summit + jnp.log(lax.optimization_barrier(jnp.sum(jnp.exp(log_stack - summit), axis=0)))
    merged_out = jnp.exp(log_list[0] - log_all)[..., None] * out_list[0]
    for branch in range(1, BRANCHES):
        merged_out = merged_out + jnp.exp(log_list[branch] - log_all)[..., None] * out_list[branch]
    return merged_out

def pack_forward(params, inputs, doc_ids):
    w_qkv, w_out, w_up, w_down, gains, shifts, hidden_bias = params
    model_width = inputs.shape[-1]
    normed = low(layer_norm(inputs, gains[0], shifts[0]))
    project = jnp.dot(normed, w_qkv, precision=highest)
    queries = low_back(low(project[:, :model_width] + shifts[1]))
    key_rows = low_back(low(project[:, model_width:2 * model_width]))
    value_rows = low_back(low(project[:, 2 * model_width:] + shifts[2]))
    shaped = (inputs.shape[0], HEADS, model_width // HEADS)
    merged_out = dilated_attention(queries.reshape(shaped), key_rows.reshape(shaped), value_rows.reshape(shaped), doc_ids)
    attended = low_back(jnp.dot(low(merged_out.reshape(inputs.shape)), w_out, precision=highest) + shifts[3])
    middle = inputs + attended
    normed_two = low(layer_norm(middle, gains[1], shifts[4]))
    hidden = low_back(jnp.dot(normed_two, w_up, precision=highest) + hidden_bias)
    active = low(jax.nn.gelu(hidden, approximate=False))
    return middle + jnp.dot(active, w_down, precision=highest) + shifts[5]

def reference(tiles, documents, cotangent, w_qkv, w_out, w_up, w_down, gains, shifts, hidden_bias):
    params = tuple((member.astype(jnp.float32) for member in (w_qkv, w_out, w_up, w_down, gains, shifts, hidden_bias)))

    def pack_step(totals, pack_item):
        inputs, doc_ids, cot_rows = pack_item
        outputs, pullback = jax.vjp(lambda param_set, pack_in: pack_forward(param_set, pack_in, doc_ids), params, inputs.astype(jnp.float32))
        param_grads, input_grads = pullback(cot_rows.astype(jnp.float32))
        totals = jax.tree.map(lambda first, second: first + second, totals, param_grads)
        return (totals, (outputs.astype(jnp.bfloat16), input_grads.astype(jnp.bfloat16)))
    zeros_init = jax.tree.map(jnp.zeros_like, params)
    totals, (encoded, grad_tiles) = lax.scan(pack_step, zeros_init, (tiles, documents, cotangent))
    return (encoded, grad_tiles, totals[0], totals[1], totals[2], totals[3], totals[4], totals[5], totals[6])
```

```python
import functools
import math

import jax
import jax.numpy as jnp
import ml_dtypes
import numpy as np
from jax import lax
from jax.experimental import pallas as pl
from jax.experimental.pallas import tpu as pltpu
from jax.sharding import PartitionSpec as P

HEADS = 16
HD = 48
D = HEADS * HD
SEG_BASE = 1024
BRANCHES = 5
T = 512
RES = 16
EPS = 1e-05
BIG = 2.0**100
SCALE = HD**-0.5
VMEM = 56 << 20
ORDER = np.array([int(f"{c:04b}"[::-1], 2) for c in range(RES)])
bf16, f32 = jnp.bfloat16, jnp.float32

VM = pl.BlockSpec(memory_space=pltpu.VMEM)
SM = pl.BlockSpec(memory_space=pltpu.SMEM)
HB = pl.BlockSpec(memory_space=pl.ANY)


def tdot(a, b):
    return lax.dot_general(a, b, (((0,), (0,)), ((), ())), preferred_element_type=f32)


def ndot(a, b):
    return lax.dot_general(a, b, (((1,), (0,)), ((), ())), preferred_element_type=f32)


def bdot(a, b):
    return lax.dot_general(a, b, (((1,), (1,)), ((), ())), preferred_element_type=f32)


def xdot(a, b):
    return lax.dot_general(a, b, (((0,), (1,)), ((), ())), preferred_element_type=f32)


def cost(us):
    return pl.CostEstimate(flops=int(us * 1e9), bytes_accessed=1000, transcendentals=0)


def kernel_call(body, in_specs, after=(), **kwargs):
    count = len(after)
    call = pl.pallas_call(
        (lambda *refs: body(*refs[count:])) if count else body,
        in_specs=[HB] * count + in_specs,
        compiler_params=pltpu.CompilerParams(vmem_limit_bytes=VMEM),
        **kwargs,
    )
    return functools.partial(call, *after)


def bit_reversed(h):
    return (h % 2) * 8 + (h // 2 % 2) * 4 + (h // 4 % 2) * 2 + h // 8


def split2(x):
    hi = x.astype(bf16)
    return hi, (x - hi.astype(f32)).astype(bf16)


def split3(x):
    a = x.astype(bf16).astype(f32)
    b = (x - a).astype(bf16).astype(f32)
    return a, b, x - a - b


def log_ratio(level):
    out = []
    for t in range(1, BRANCHES):
        c = math.log2((t + 1 - level) / (t - level)) if t > level else 0.0
        hi = float(np.asarray(c).astype(ml_dtypes.bfloat16))
        out.append((hi, float(np.asarray(c - hi).astype(ml_dtypes.bfloat16))))
    return out


def valuation(g, pos):
    c = pos >> 5
    hits = [((c >> n) == (g >> n)).astype(jnp.int32) for n in (3, 2, 1, 0)]
    return hits[0] + hits[1] + hits[2] + hits[3]


def query_side(g, q, docs, pos, level, lm=None):
    n = q.shape[1]
    hi, lo = split2(q.astype(f32) * (SCALE * math.log2(math.e)))
    row = lax.broadcasted_iota(jnp.int32, (32, n), 0)
    v = valuation(g, pos)
    f = jnp.where((row < 4) & (row == docs), -BIG, 0.0)
    for i, parts in enumerate(log_ratio(level)):
        for j, part in enumerate(parts):
            if part:
                f = jnp.where((row == 4 + 2 * i + j) & (v > i), part, f)
    if level >= 3:
        f = jnp.where(row == 12, -BIG, f)
    if level >= 4:
        f = jnp.where(row == 13, -BIG, f)
    if lm is not None:
        for r, part in enumerate(split3(lm)):
            f = jnp.where(row == 14 + r, -part, f)
    return jnp.concatenate([hi, lo, f.astype(bf16)], axis=0)


def key_side(g, k, docs):
    n = k.shape[1]
    pos = lax.broadcasted_iota(jnp.int32, (1, n), 1) & (T - 1)
    row = lax.broadcasted_iota(jnp.int32, (32, n), 0)
    v = valuation(g, pos)
    f = jnp.where((row < 4) & (row != docs), 1.0, 0.0)
    f = jnp.where((row >= 4) & (row < 12) & (v >= ((row - 2) >> 1)), 1.0, f)
    f = jnp.where((row == 12) & (v < 3), 1.0, f)
    f = jnp.where((row == 13) & (v < 4), 1.0, f)
    f = jnp.where((row >= 14) & (row < 17), 1.0, f)
    return jnp.concatenate([k, k, f.astype(bf16)], axis=0)


def ones_below(v, count):
    row = lax.broadcasted_iota(jnp.int32, (16, v.shape[1]), 0)
    return jnp.concatenate([v, jnp.where(row < count, 1.0, 0.0).astype(bf16)], axis=0)


def positions(first, n, width):
    return first + (lax.broadcasted_iota(jnp.int32, (1, n), 1) & (width - 1))


def attend(jobs):
    scores = [tdot(kf, qf) for kf, _, qf in jobs]
    tops = [jnp.max(s, axis=0, keepdims=True) for s in scores]
    weights = [jnp.exp2(s - m).astype(bf16) for s, m in zip(scores, tops)]
    outs = [ndot(v1, p) for (_, v1, _), p in zip(jobs, weights)]
    return [(o[:HD] * (1.0 / o[HD : HD + 1]), m + jnp.log2(o[HD : HD + 1])) for o, m in zip(outs, tops)]


def attend_back(jobs):
    weights = [jnp.exp2(tdot(kf, qf)) for kf, _, _, qf, _, _ in jobs]
    slopes = [tdot(v3, gf) for _, _, v3, _, _, gf in jobs]
    ds = [(p * dp).astype(bf16) for p, dp in zip(weights, slopes)]
    ps = [p.astype(bf16) for p in weights]
    return [(ndot(k, d), bdot(q, d), bdot(gf[:HD], p)) for (_, k, _, _, q, gf), d, p in zip(jobs, ds, ps)]


def gradient_side(grad, dd):
    row = lax.broadcasted_iota(jnp.int32, (16, grad.shape[1]), 0)
    f = jnp.zeros((16, grad.shape[1]), f32)
    for r, part in enumerate(split3(dd)):
        f = jnp.where(row == r, -part, f)
    return jnp.concatenate([grad, f.astype(bf16)], axis=0)


TILE = 256
TILES = [slice(at, at + TILE) for at in range(0, T, TILE)]


def head_of(ref, i, rows=HD):
    return ref[i * rows : (i + 1) * rows]


def near_kernel(q_ref, k_ref, v_ref, docs_ref, o_ref, lm_ref):
    docs = docs_ref[...]
    jobs = []
    for i in range(NEAR):
        g = pl.program_id(0) * NEAR + i
        kf = key_side(g, head_of(k_ref, i), docs)
        v1 = ones_below(head_of(v_ref, i), 1)
        q = head_of(q_ref, i)
        jobs += [(kf, v1, query_side(g, q[:, c], docs[:, c], positions(c.start, TILE, T), 0)) for c in TILES]
    done = attend(jobs)
    for i in range(NEAR):
        for c in TILES:
            o, lm = done.pop(0)
            o_ref[i * HD : (i + 1) * HD, c] = o
            lm_ref[i, :, c] = lm


def window(ref, g, level):
    w = T >> min(level, 2)
    at = pl.multiple_of((g >> (4 - min(level, 2))) * w, 128)
    return jnp.concatenate([ref[:, pl.ds(at, w)], ref[:, pl.ds(T + at, w)]], axis=1)


def guest_side(g, level, q, docs_ref, lm=None):
    width = T >> level
    block = g >> (4 - level)
    rows = docs_ref[...].astype(f32)
    pick = lax.broadcasted_iota(jnp.int32, rows.shape, 0) == block
    docs = jnp.sum(jnp.where(pick, rows, 0.0), axis=0, keepdims=True).astype(jnp.int32)
    return query_side(g, q, docs, positions(block * width, q.shape[1], width), level, lm)


def stat_rows(rows):
    parts = [p for row in rows for p in split3(row)]
    return jnp.concatenate(parts + [jnp.zeros((16 - len(parts), rows[0].shape[1]), f32)], axis=0).astype(bf16)


def stat_row(block, i):
    rows = block[HD + 3 * i : HD + 3 * i + 3].astype(f32)
    return rows[0:1] + rows[1:2] + rows[2:3]


def far_kernel(levels, k_ref, v_ref, docs_ref, *refs):
    kf_ref = refs[-1]
    ins, outs = refs[: 2 * len(levels)], refs[2 * len(levels) : -1]
    jobs = []
    for i in range(FAR):
        g = pl.program_id(0) * FAR + i
        kf_ref[i] = key_side(g, head_of(k_ref, i), docs_ref[...])
        rows = pl.ds(i * HD, HD)
        for j, level in enumerate(levels):
            qf = guest_side(g, level, head_of(ins[2 * j], i), ins[2 * j + 1])
            jobs.append((window(kf_ref.at[i], g, level), ones_below(window(v_ref.at[rows], g, level), 1), qf))
    done = attend(jobs)
    for i in range(FAR):
        for out in outs:
            o, lm = done.pop(0)
            out[i * ROWS : (i + 1) * ROWS] = jnp.concatenate([o.astype(bf16), stat_rows([lm])], axis=0)


def near_back_kernel(first, q_ref, k_ref, v_ref, docs_ref, g_ref, lm_ref, dd_ref, *refs):
    gq_ref, gk_ref, gv_ref = refs[-3:]
    docs = docs_ref[...]
    jobs = []
    for i in range(NEAR):
        g = pl.program_id(0) * NEAR + i + first
        k, q, grad, lm, dd = head_of(k_ref, i), head_of(q_ref, i), head_of(g_ref, i), lm_ref[i], dd_ref[i]
        kf = key_side(g, k, docs)
        v3 = ones_below(head_of(v_ref, i), 3)
        for c in TILES:
            qf = query_side(g, q[:, c], docs[:, c], positions(c.start, TILE, T), 0, lm[:, c])
            jobs.append((kf, k, v3, qf, q[:, c], gradient_side(grad[:, c], dd[:, c])))
    done = attend_back(jobs)
    for i in range(NEAR):
        rows = slice(i * HD, (i + 1) * HD)
        mine = [done.pop(0) for _ in TILES]
        for c, (dq, _, _) in zip(TILES, mine):
            gq_ref[rows, c] = (dq * SCALE).astype(bf16)
        gk_ref[rows] = (sum(d[1] for d in mine) * SCALE).astype(bf16)
        gv_ref[rows] = sum(d[2] for d in mine).astype(bf16)


def far_back_kernel(levels, k_ref, v_ref, docs_ref, *refs):
    kf_ref, ak_ref, av_ref = refs[-3:]
    n = len(levels)
    ins, outs = refs[: 3 * n], refs[3 * n : -3]
    jobs = []
    for i in range(FAR):
        g = pl.program_id(0) * FAR + i
        kf_ref[i] = key_side(g, head_of(k_ref, i), docs_ref[...])
        rows = pl.ds(i * HD, HD)
        for j, level in enumerate(levels):
            q_ref, dq_ref, g_ref = ins[3 * j : 3 * j + 3]
            q, grad = head_of(q_ref, i), head_of(g_ref, i, ROWS)
            qf = guest_side(g, level, q, dq_ref, stat_row(grad, 0))
            gf = gradient_side(grad[:HD], stat_row(grad, 1))
            k, v = window(k_ref.at[rows], g, level), window(v_ref.at[rows], g, level)
            jobs.append((window(kf_ref.at[i], g, level), k, ones_below(v, 3), qf, q, gf))
    done = attend_back(jobs)
    ak_ref[...] = jnp.zeros_like(ak_ref)
    av_ref[...] = jnp.zeros_like(av_ref)
    for i in range(FAR):
        g = pl.program_id(0) * FAR + i
        rows = slice(i * HD, (i + 1) * HD)
        for j, level in enumerate(levels):
            dq, dk, dv = done.pop(0)
            outs[2 + j][rows] = (dq * SCALE).astype(bf16)
            w = T >> min(level, 2)
            at = (g >> (4 - min(level, 2))) * w
            for c in range(2):
                cols = pl.ds(pl.multiple_of(c * T + at, 128), w)
                ak_ref[rows, cols] += dk[:, c * w : (c + 1) * w]
                av_ref[rows, cols] += dv[:, c * w : (c + 1) * w]
    outs[0][...] = (ak_ref[...] * SCALE).astype(bf16)
    outs[1][...] = av_ref[...].astype(bf16)


NEAR, FAR = 2, 4
ROWS = 64


def head_rows(n, heads, first=0, rows=HD):
    return pl.BlockSpec((rows * heads, n), lambda i: (i + first // heads, 0))


def head_stats(n, heads, first=0):
    return pl.BlockSpec((heads, 1, n), lambda i: (i + first // heads, 0, 0))


def whole(*shape):
    return pl.BlockSpec(shape, lambda i: (0,) * len(shape))


def guest_docs(n):
    return pl.BlockSpec((16, n), lambda i: (D // 16, 0))


def shape_of(*dims, dtype=bf16):
    return jax.ShapeDtypeStruct(dims, dtype)


def attend_near(q, k, v, docs):
    r = lambda n: head_rows(n, NEAR)
    return kernel_call(
        near_kernel,
        grid=(HEADS // NEAR,),
        in_specs=[r(T), r(2 * T), r(2 * T), whole(1, 2 * T)],
        out_specs=[r(T), head_stats(T, NEAR)],
        out_shape=[shape_of(D, T, dtype=f32), shape_of(HEADS, 1, T, dtype=f32)],
        cost_estimate=cost(1),
        name="near",
    )(q, k, v, docs)


def attend_far(k, v, docs, guests, after):
    r = lambda n: head_rows(n, FAR)
    in_specs = [r(2 * T), r(2 * T), whole(1, 2 * T)]
    out_specs, out_shape, args = [], [], []
    for level, q in guests:
        n = q.shape[1]
        in_specs += [r(n), guest_docs(n)]
        out_specs.append(head_rows(n, FAR, 0, ROWS))
        out_shape.append(shape_of(ROWS * HEADS, n))
        args += [q, q]
    return kernel_call(
        functools.partial(far_kernel, [v[0] for v in guests]),
        after=after,
        grid=(HEADS // FAR,),
        in_specs=in_specs,
        out_specs=out_specs,
        out_shape=out_shape,
        scratch_shapes=[pltpu.VMEM((FAR, 128, 2 * T), bf16)],
        cost_estimate=cost(1),
        name="far",
    )(k, v, docs, *args)


def near_back(q, k, v, docs, grads, lm, dd, first, count, rest=(), after=()):
    r = lambda n: head_rows(n, NEAR, first)
    return kernel_call(
        functools.partial(near_back_kernel, first),
        after=after,
        grid=(count // NEAR,),
        in_specs=[r(T), r(2 * T), r(2 * T), whole(1, 2 * T), r(T), head_stats(T, NEAR, first), head_stats(T, NEAR, first)] + [HB] * len(rest),
        out_specs=[r(T), r(2 * T), r(2 * T)],
        out_shape=[shape_of(D, n) for n in (T, 2 * T, 2 * T)],
        input_output_aliases={len(after) + 7 + i: i for i in range(len(rest))},
        cost_estimate=cost(1),
        name="near_back",
    )(q, k, v, docs, grads, lm, dd, *rest)


def far_back(k, v, docs, guests, after):
    r = lambda n: head_rows(n, FAR)
    in_specs = [r(2 * T), r(2 * T), whole(1, 2 * T)]
    out_specs, out_shape, args = [r(2 * T)] * 2, [shape_of(D, 2 * T)] * 2, []
    for level, q, grads in guests:
        n = q.shape[1]
        in_specs += [r(n), guest_docs(n), head_rows(n, FAR, 0, ROWS)]
        out_specs.append(r(n))
        out_shape.append(shape_of(D, n))
        args += [q, q, grads]
    return kernel_call(
        functools.partial(far_back_kernel, [v[0] for v in guests]),
        after=after,
        grid=(HEADS // FAR,),
        in_specs=in_specs,
        out_specs=out_specs,
        out_shape=out_shape,
        scratch_shapes=[pltpu.VMEM((FAR, 128, 2 * T), bf16), pltpu.VMEM((FAR * HD, 2 * T), f32), pltpu.VMEM((FAR * HD, 2 * T), f32)],
        cost_estimate=cost(1),
        name="far_back",
    )(k, v, docs, *args)


def permutation():
    p = lax.broadcasted_iota(jnp.int32, (T, T), 0)
    o = lax.broadcasted_iota(jnp.int32, (T, T), 1)
    return jnp.where(o == p % 32 * RES + bit_reversed(p // 32), 1.0, 0.0).astype(bf16)


def normalized(x):
    center = jnp.mean(x, axis=-1, keepdims=True)
    centered = x - center
    rstd = lax.rsqrt(jnp.mean(centered * centered, axis=-1, keepdims=True) + EPS)
    return centered * rstd, rstd


def norm_pullback(grad, xhat, rstd, gain):
    g = grad * gain
    gx = rstd * (g - jnp.mean(g, axis=-1, keepdims=True) - xhat * jnp.mean(g * xhat, axis=-1, keepdims=True))
    return gx, jnp.sum(grad * xhat, axis=0, keepdims=True), jnp.sum(grad, axis=0, keepdims=True)


def fetch(shards, buffer, sems, where_ref, rows):
    out = []
    for r, shard in enumerate(shards):
        at = pl.multiple_of(where_ref[r] * rows, rows)
        out.append(pltpu.make_async_copy(shard.at[pl.ds(0, rows)], buffer.at[pl.ds(at, rows)], sems.at[r]))
        out[-1].start()
    return out


def add_bias(values, row_ref, r):
    pick = jnp.where(lax.broadcasted_iota(jnp.int32, (16, values.shape[1]), 0) == r, 1.0, 0.0).astype(bf16)
    return values + tdot(row_ref, pick)


def block_lanes(g, level):
    at = g // (RES >> level) * (T >> level)
    return slice(at, at + (T >> level))


def head_slice(g):
    return slice(g * HD, (g + 1) * HD)


def project_kernel(levels, where_ref, w0, w1, w2, w3, vec_ref, bias_ref, docs_ref, x0_ref, x1_ref, *refs):
    q_ref, k_ref, v_ref, n_ref, in_ref, dout_ref = refs[:6]
    visit_refs = refs[6 : 5 + levels]
    w_ref, wt_ref, sems = refs[5 + levels :]
    copies = fetch((w0, w1, w2, w3), w_ref, sems, where_ref, D // 4)
    perm = permutation()
    gain, shift = vec_ref[0:1], vec_ref[2:3]

    def norm(x):
        xhat, _ = normalized(x.astype(f32))
        return ndot(perm, (xhat * gain + shift).astype(bf16)).astype(bf16)

    in_ref[...] = ndot(perm, x0_ref[...]).astype(bf16)
    n_ref[:T] = norm(x0_ref[...])
    n_ref[T:] = norm(x1_ref[:T])
    own_docs = bdot(jnp.broadcast_to(docs_ref[...].astype(f32), (8, T)).astype(bf16), perm)[0:1]
    near_docs = bdot(x1_ref[T:, :T], perm)[0:1]
    dout_ref[...] = jnp.concatenate([own_docs, near_docs], axis=1).astype(jnp.int32)
    for c in copies:
        c.wait()
    for part in range(3):
        wt = w_ref[:, part * D : (part + 1) * D].T
        for g in range(HEADS):
            h = int(ORDER[g])
            wt_ref[part * D + g * HD : part * D + (g + 1) * HD, :] = wt[head_slice(h)]
    n = n_ref[...]
    q_ref[...] = add_bias(bdot(wt_ref[:D, :], n_ref[:T]), bias_ref[...], 0).astype(bf16)
    for level in range(1, levels):
        width = T >> level
        visit = visit_refs[level - 1]
        for g in range(HEADS):
            visit[head_slice(g), :] = q_ref[head_slice(g), block_lanes(g, level)]
        rows = [own_docs[:, b * width : (b + 1) * width] for b in range(1 << level)]
        if level < 4:
            rows.append(jnp.zeros((16 - len(rows), width), f32))
        visit[D:, :] = jnp.concatenate(rows, axis=0).astype(bf16)
    k_ref[...] = bdot(wt_ref[D : 2 * D, :], n).astype(bf16)
    v_ref[...] = add_bias(bdot(wt_ref[2 * D :, :], n), bias_ref[...], 1).astype(bf16)


def project(levels, where, shards, vectors, biases, docs, tile, tile_near):
    return kernel_call(
        functools.partial(project_kernel, levels),
        in_specs=[SM] + [HB] * 4 + [VM] * 5,
        out_specs=[VM] * (5 + levels),
        out_shape=[shape_of(D, T), shape_of(D, 2 * T), shape_of(D, 2 * T), shape_of(2 * T, D), shape_of(T, D), shape_of(1, 2 * T, dtype=jnp.int32)]
        + [shape_of(D + 16, T >> level) for level in range(1, levels)],
        scratch_shapes=[pltpu.VMEM((D, 3 * D), bf16), pltpu.VMEM((3 * D, D), bf16), pltpu.SemaphoreType.DMA((4,))],
        cost_estimate=cost(1),
        name="project",
    )(where, *shards, vectors, biases, docs, tile, tile_near)


ERF_TOP = (0.00022905065861350646, 0.0034082910107109506, 0.050955695062380861, 0.18520832239976145, 1.128379143519084)
ERF_BOTTOM = (-1.1791602954361697e-7, 0.000023547966471313185, 0.0010179625278914885, 0.014070470171167667, 0.11098505178285362, 0.49746925110067538, 1.0)


def erf(x):
    x = jnp.clip(x, -3.7439211627767994, 3.7439211627767994)
    y = x * x
    top, bottom = ERF_TOP[0], ERF_BOTTOM[0]
    for c in ERF_TOP[1:]:
        top = top * y + c
    for c in ERF_BOTTOM[1:]:
        bottom = bottom * y + c
    return x * top / bottom


FF_PART = 768
FF_ROWS = 2 * FF_PART + D // 4


def merge_heads(o_ref, lm_ref, back, merged_ref, lmf_ref):
    for g in range(HEADS):
        base = lm_ref[g]
        parts, top = [], base
        blocks = [head_of(ref, g, ROWS) for _, ref in back]
        for (level, _), block in zip(back, blocks):
            cols = block_lanes(g, level)
            rest = [jnp.full((1, n), -BIG, f32) for n in (cols.start, T - cols.stop)]
            parts.append(jnp.concatenate([x for x in (rest[0], stat_row(block, 0), rest[1]) if x.shape[1]], axis=1))
            top = jnp.maximum(top, parts[-1])
        weights = [jnp.exp2(x - top) for x in [base] + parts]
        total = sum(weights)
        scale = 1.0 / total
        out = o_ref[head_slice(g), :] * (weights[0] * scale)
        for (level, _), block, w in zip(back, blocks, weights[1:]):
            cols = block_lanes(g, level)
            add = block[:HD].astype(f32) * (w * scale)[:, cols]
            rest = [jnp.zeros((HD, n), f32) for n in (cols.start, T - cols.stop)]
            out = out + jnp.concatenate([x for x in (rest[0], add, rest[1]) if x.shape[1]], axis=1)
        merged_ref[head_slice(int(ORDER[g])), :] = out
        lmf_ref[g] = top + jnp.log2(total)


def middle_kernel(levels, back_levels, where_ref, *refs):
    shards, refs = refs[:4], refs[4:]
    o_ref, lm_ref, in_ref, cot_ref, vec_ref, hb_ref = refs[:6]
    n = len(back_levels)
    back = list(zip(back_levels, refs[6 : 6 + n]))
    refs = refs[6 + n :]
    enc_ref, mine_out, theirs_out, gm_ref, dd_ref, lmf_ref, gmid_ref, small_ref, gbias_ref = refs[:9]
    grad_out = lambda r, at, rows: (mine_out, theirs_out)[r % 2].at[r // 2, pl.ds(at, rows)]
    visit_refs, refs = refs[9 : 8 + levels], refs[8 + levels :]
    wo_ref, wu_ref, wd_ref, gd_ref, gu_ref, act_ref, merged_ref, y_ref, gn_ref, gy_ref, n2_ref, sems, osems = refs
    out_copies = fetch(shards, wo_ref, sems.at[0], where_ref, D // 4)
    up_copies, down_copies = [], []
    for r, shard in enumerate(shards):
        rows = pl.ds(pl.multiple_of(where_ref[r] * (D // 4), D // 4), D // 4)
        for c in range(4):
            dst = wu_ref.at[rows, pl.ds(c * FF_PART, FF_PART)]
            up_copies.append(pltpu.make_async_copy(shard.at[pl.ds((1 + c) * (D // 4), D // 4)], dst, sems.at[1 + c, r]))
            up_copies[-1].start()
    for r, shard in enumerate(shards):
        down_copies.append(pltpu.make_async_copy(shard.at[pl.ds(5 * (D // 4), FF_PART)], wd_ref.at[r], sems.at[5, r]))
        down_copies[-1].start()
    perm = permutation()
    gy_ref[...] = ndot(perm, cot_ref[...]).astype(bf16)
    merge_heads(o_ref, lm_ref, back, merged_ref, lmf_ref)
    merged = merged_ref[...].astype(bf16)
    for c in out_copies:
        c.wait()
    middle = in_ref[...].astype(f32) + tdot(merged, wo_ref[...]) + vec_ref[5:6]
    xhat, rstd = normalized(middle)
    n2_ref[...] = (xhat * vec_ref[1:2] + vec_ref[6:7]).astype(bf16)
    y_ref[...] = middle + vec_ref[7:8]
    gn_ref[...] = jnp.zeros_like(gn_ref)
    for c in up_copies:
        c.wait()
    down_parts = []
    for r in range(4):
        at = pl.multiple_of(where_ref[r] * FF_PART, FF_PART)
        cols = pl.ds(at, FF_PART)
        down_copies[r].wait()
        n2, gy = n2_ref[...], gy_ref[...]
        hidden = ndot(n2, wu_ref[:, cols]) + hb_ref[:, cols]
        phi = 0.5 + 0.5 * erf(hidden * 0.5**0.5)
        slope = phi + hidden * (jnp.exp(hidden * hidden * -0.5) * (2 * math.pi) ** -0.5)
        active = (hidden * phi).astype(bf16)
        y_ref[...] += ndot(active, wd_ref[r])
        gd_ref[r] = tdot(active, gy).astype(bf16)
        down_parts.append(pltpu.make_async_copy(gd_ref.at[r], grad_out(r, 0, FF_PART), osems.at[r]))
        down_parts[-1].start()
        gh = (slope * bdot(gy, wd_ref[r])).astype(bf16)
        gbias_ref[:, cols] = jnp.sum(gh.astype(f32), axis=0, keepdims=True)
        gu_ref[:, cols] = tdot(n2, gh).astype(bf16)
        gn_ref[...] += bdot(gh, wu_ref[:, cols])
    up_parts = []
    for r in range(4):
        at = pl.multiple_of(where_ref[r] * (D // 4), D // 4)
        for c in range(4):
            src = gu_ref.at[pl.ds(at, D // 4), pl.ds(c * FF_PART, FF_PART)]
            up_parts.append(pltpu.make_async_copy(src, grad_out(r, FF_PART + (1 + c) * (D // 4), D // 4), osems.at[8 + 4 * r + c]))
            up_parts[-1].start()
    enc_ref[...] = tdot(perm, y_ref[...].astype(bf16)).astype(bf16)
    gy = gy_ref[...].astype(f32)
    middle = in_ref[...].astype(f32) + tdot(merged, wo_ref[...]) + vec_ref[5:6]
    xhat, rstd = normalized(middle)
    gx, ggain, gshift = norm_pullback(gn_ref[...], xhat, rstd, vec_ref[1:2])
    gmid = gy + gx
    gmid_ref[...] = gmid
    gatt = gmid.astype(bf16)
    act_ref[...] = ndot(merged, gatt).astype(bf16)
    for r in range(4):
        at = pl.multiple_of(where_ref[r] * (D // 4), D // 4)
        down_parts.append(pltpu.make_async_copy(act_ref.at[pl.ds(at, D // 4)], grad_out(r, FF_PART, D // 4), osems.at[4 + r]))
        down_parts[-1].start()
    gm = bdot(wo_ref[...], gatt)
    prod = gm * merged_ref[...]
    gm = gm.astype(bf16)
    for g in range(HEADS):
        h = head_slice(int(ORDER[g]))
        gm_ref[head_slice(g), :] = gm[h]
        dd = jnp.sum(prod[h], axis=0, keepdims=True)
        dd_ref[g] = dd
        for level in range(1, levels):
            cols = block_lanes(g, level)
            block = jnp.concatenate([gm[h, cols], stat_rows([lmf_ref[g][:, cols], dd[:, cols]])], axis=0)
            visit_refs[level - 1][g * ROWS : (g + 1) * ROWS] = block
    zero = jnp.zeros((4, D), f32)
    small_ref[...] = jnp.concatenate(
        [ggain, jnp.sum(gatt.astype(f32), axis=0, keepdims=True), gshift, jnp.sum(gy, axis=0, keepdims=True), zero], axis=0)
    for c in down_parts + up_parts:
        c.wait()


def middle(levels, where, shards, o, lm, back, inputs, cotangent, vectors, bias):
    s = shape_of
    ff = bias.shape[1]
    visits = [s(ROWS * HEADS, T >> level) for level in range(1, levels)]
    return kernel_call(
        functools.partial(middle_kernel, levels, [b[0] for b in back]),
        in_specs=[SM] + [HB] * 4 + [VM] * (6 + len(back)),
        out_specs=[VM] + [HB] * 2 + [VM] * (6 + len(visits)),
        out_shape=[
            s(T, D), s(2, FF_ROWS, D), s(2, FF_ROWS, D),
            s(D, T), s(HEADS, 1, T, dtype=f32), s(HEADS, 1, T, dtype=f32), s(T, D, dtype=f32), s(8, D, dtype=f32), s(1, ff, dtype=f32),
        ] + visits,
        scratch_shapes=[
            pltpu.VMEM((D, D), bf16), pltpu.VMEM((D, ff), bf16), pltpu.VMEM((4, FF_PART, D), bf16),
            pltpu.VMEM((4, FF_PART, D), bf16), pltpu.VMEM((D, ff), bf16), pltpu.VMEM((D, D), bf16), pltpu.VMEM((D, T), f32),
            pltpu.VMEM((T, D), f32), pltpu.VMEM((T, D), f32), pltpu.VMEM((T, D), bf16), pltpu.VMEM((T, D), bf16),
            pltpu.SemaphoreType.DMA((6, 4)), pltpu.SemaphoreType.DMA((24,)),
        ],
        cost_estimate=cost(1),
        name="middle",
    )(where, *shards, o, lm, inputs, cotangent, vectors, bias, *[b[1] for b in back])


def natural(refs):
    rows = []
    for h in range(HEADS):
        g = head_slice(int(ORDER[h]))
        rows.append(sum(ref[g, :].astype(f32) for ref in refs).astype(bf16))
    return jnp.concatenate(rows, axis=0)


def to_blocks(where_ref, src_ref, out_refs, parts):
    rows = D // 4
    for r in range(4):
        at = pl.multiple_of(where_ref[r] * rows, rows)
        for part in range(parts):
            out_refs[r % 2][r // 2, part * rows : (part + 1) * rows, :] = src_ref[pl.ds(at, rows), part * D : (part + 1) * D]


def keys_kernel(where_ref, w0, w1, w2, w3, nk_ref, nv_ref, fk_ref, fv_ref, n_ref,
                send_ref, own_ref, mine_ref, theirs_ref, sums_ref, w_ref, gp_ref, gw_ref, sems):
    copies = fetch((w0, w1, w2, w3), w_ref, sems, where_ref, D // 4)
    gp_ref[:D] = natural((nk_ref, fk_ref))
    gp_ref[D:] = natural((nv_ref, fv_ref))
    for c in copies:
        c.wait()
    send_ref[...] = xdot(gp_ref[:, T:], w_ref[:, D:]).astype(bf16)
    gw_ref[...] = xdot(n_ref[...], gp_ref[...]).astype(bf16)
    to_blocks(where_ref, gw_ref, (mine_ref, theirs_ref), 2)
    own_ref[...] = xdot(gp_ref[:, :T], w_ref[:, D:])
    sums_ref[...] = bdot(jnp.ones((16, 2 * T), bf16), gp_ref[D:, :])[:8]


def keys_last(where, shards, grads, normed, after):
    s = shape_of
    return kernel_call(
        keys_kernel,
        after=after,
        in_specs=[SM] + [HB] * 4 + [VM] * 5,
        out_specs=[VM] * 5,
        out_shape=[s(T, D), s(T, D, dtype=f32), s(2, D // 2, D), s(2, D // 2, D), s(8, D, dtype=f32)],
        scratch_shapes=[pltpu.VMEM((D, 3 * D), bf16), pltpu.VMEM((2 * D, 2 * T), bf16), pltpu.VMEM((D, 2 * D), bf16), pltpu.SemaphoreType.DMA((4,))],
        cost_estimate=cost(1),
        name="keys_last",
    )(where, *shards, *grads, normed)


LAST_ROWS = 256


def last_kernel(back_levels, where_ref, w0, w1, w2, w3, gq_ref, *refs):
    back = list(zip(back_levels, refs))
    n_ref, in_ref, gmid_ref, vec_ref, small_ref, gbias_ref, own_ref, got_ref, sums_ref, gt_ref, mine_ref, theirs_ref = refs[len(back) : len(back) + 12]
    w_ref, gp_ref, gw_ref, sems = refs[len(back) + 12 :]
    copies = fetch((w0, w1, w2, w3), w_ref, sems, where_ref, D // 4)
    for g in range(HEADS):
        rows = head_slice(g)
        total = gq_ref[rows, :].astype(f32)
        for level, ref in back:
            cols = block_lanes(g, level)
            rest = [jnp.zeros((HD, n), f32) for n in (cols.start, T - cols.stop)]
            total = total + jnp.concatenate([x for x in (rest[0], ref[rows, :].astype(f32), rest[1]) if x.shape[1]], axis=1)
        gp_ref[head_slice(int(ORDER[g])), :] = total.astype(bf16)
    gw_ref[...] = xdot(n_ref[:T], gp_ref[...]).astype(bf16)
    to_blocks(where_ref, gw_ref, (mine_ref, theirs_ref), 1)
    sums = bdot(jnp.ones((16, T), bf16), gp_ref[...])
    for c in copies:
        c.wait()
    grad = xdot(gp_ref[...], w_ref[:, :D]) + own_ref[...] + got_ref[...].astype(f32)
    xhat, rstd = normalized(in_ref[...].astype(f32))
    gx, ggain, gshift = norm_pullback(grad, xhat, rstd, vec_ref[0:1])
    rows = [ggain, small_ref[0:1], gshift, sums[0:1], sums_ref[0:1], small_ref[1:4]]
    rows += [gbias_ref[:, i * D : (i + 1) * D] for i in range(4)]
    rows += [jnp.zeros((4, D), f32)]
    small = jnp.concatenate(rows, axis=0).astype(bf16)
    for out in (mine_ref, theirs_ref):
        for r in range(2):
            out[r, D // 4 : D // 4 + 16, :] = small
            out[r, D // 4 + 16 :, :] = jnp.zeros((LAST_ROWS - D // 4 - 16, D), bf16)
    gt_ref[...] = tdot(permutation(), (gmid_ref[...] + gx).astype(bf16)).astype(bf16)


def last(where, shards, gq, back, normed, inputs, gmid, vectors, small, gbias, own, got, sums, after):
    return kernel_call(
        functools.partial(last_kernel, [b[0] for b in back]),
        after=after,
        in_specs=[SM] + [HB] * 4 + [VM] * (10 + len(back)),
        out_specs=[VM] * 3,
        out_shape=[shape_of(T, D), shape_of(2, LAST_ROWS, D), shape_of(2, LAST_ROWS, D)],
        scratch_shapes=[pltpu.VMEM((D, 3 * D), bf16), pltpu.VMEM((D, T), bf16), pltpu.VMEM((D, D), bf16), pltpu.SemaphoreType.DMA((4,))],
        cost_estimate=cost(1),
        name="last",
    )(where, *shards, gq, *[b[1] for b in back], normed, inputs, gmid, vectors, small, gbias, own, got, sums)


def exchanged(x, axis, mask):
    return lax.ppermute(x, axis, [(i, i ^ mask) for i in range(lax.axis_size(axis))])


def added(a, b):
    return (a.astype(f32) + b.astype(f32)).astype(bf16)


def behind(x, other):
    return lax.optimization_barrier((x, other))[0]


def core_sum(mine, theirs):
    return added(mine, exchanged(theirs, "fsdp", 1))


def halved(x, rank, bit):
    half = x.shape[1] // 2
    mine = rank >> bit & 1
    kept = lax.dynamic_slice_in_dim(x, mine * half, half, 1)
    sent = lax.dynamic_slice_in_dim(x, (1 - mine) * half, half, 1)
    return added(kept, exchanged(sent, "seq", 1 << bit))


def doubled(x, rank, bit):
    theirs = exchanged(x, "seq", 1 << bit)
    low = (rank >> bit & 1) == 0
    return jnp.concatenate([jnp.where(low, x, theirs), jnp.where(low, theirs, x)], axis=1)


def chip_sum(x):
    return added(x[:1], exchanged(x[1:], "fsdp", 2))


def beyond(x, seq):
    for bit in range(3, seq.bit_length() - 1):
        x = added(x, exchanged(x, "seq", 1 << bit))
    return x


def direct(mine, theirs, seq):
    pair = core_sum(mine, theirs)
    own = added(pair[0], exchanged(pair[1], "fsdp", 2))
    pieces = lax.all_to_all(own.reshape(seq, -1, D), "seq", 0, 0)
    piece = jnp.sum(pieces.astype(f32), axis=0).astype(bf16)
    return lax.all_to_all(jnp.broadcast_to(piece[None], (seq,) + piece.shape), "seq", 0, 0).reshape(-1, D)


def local(tiles, documents, cotangent, w_qkv, w_out, w_up, w_down, gains, shifts, hidden_bias):
    seq = lax.axis_size("seq")
    rank = lax.axis_index("seq")
    part = lax.axis_index("fsdp")
    levels = min(BRANCHES, (seq * T // SEG_BASE).bit_length())
    where = jnp.stack([part ^ r for r in range(4)]).astype(jnp.int32)
    visits = [(level, (1 << level) + 2 * c) for level in range(1, levels) for c in range(1 << level - 1)]
    cols = gains.shape[1]

    packed = jnp.concatenate([gains, shifts, hidden_bias.reshape(-1, cols)], axis=0).reshape(1, -1)
    w_ext = jnp.concatenate([w_qkv, jnp.pad(packed, ((0, 7), (0, 0)))], axis=0)
    qkv_far = exchanged(w_ext, "fsdp", 2)
    tile = tiles[0]
    docs_row = jnp.pad(documents.astype(bf16), ((0, 7), (0, D - T)))
    tile_near = exchanged(jnp.concatenate([tile, docs_row], axis=0), "seq", 1)
    stacked_up = w_up.reshape(cols, -1, D).swapaxes(0, 1).reshape(-1, D)
    w_ff = jnp.concatenate([w_out, stacked_up, w_down], axis=0)
    ff_far = exchanged(w_ff, "fsdp", 2)
    qkv_near = exchanged(w_ext, "fsdp", 1)
    qkv_shards = (w_ext, qkv_near, qkv_far, exchanged(behind(qkv_far, tile_near), "fsdp", 1))
    ff_near = exchanged(w_ff, "fsdp", 1)

    stacked = jnp.stack([w[cols].reshape(-1, cols) for w in qkv_shards])
    in_order = jnp.stack([lax.dynamic_index_in_dim(stacked, part ^ s, 0, keepdims=False) for s in range(4)])
    rows = in_order[:, :8].transpose(1, 0, 2).reshape(8, D)
    vectors = rows.astype(f32)
    bias_row = in_order[:, 8:].reshape(1, -1).astype(f32)
    by_head = rows[3:5].reshape(2, 2, 2, 2, 2, HD).transpose(0, 4, 3, 2, 1, 5).reshape(2, D)
    biases = jnp.concatenate([by_head, jnp.zeros((14, D), bf16)], axis=0)

    q, k, v, normed, inputs, docs, *queries = project(levels, where, qkv_shards, vectors, biases, documents, tile, tile_near)
    guests = [(level, exchanged(queries[level - 1], "seq", mask)) for level, mask in visits]
    o, lm = attend_near(q, k, v, docs)
    partial = attend_far(k, v, docs, guests, [lm])
    back = [(level, exchanged(x, "seq", mask)) for (level, mask), x in zip(visits, partial)]
    shards = (w_ff, ff_near, ff_far, exchanged(behind(ff_far, back[1][1]), "fsdp", 1))

    encoded, early_mine, early_theirs, gmerged, dd, lmf, gmid, small, gbias, *send = middle(
        levels, where, shards, o, lm, back, inputs, cotangent[0], vectors, bias_row)

    early_theirs = exchanged(early_theirs, "fsdp", 1)
    guests = [guest + (exchanged(send[level - 1], "seq", mask),) for guest, (level, mask) in zip(guests, visits)]
    nears = near_back(q, k, v, docs, gmerged, lmf, dd, 0, 8)
    early = added(early_mine, behind(early_theirs, nears[0]))
    n = FF_PART + D // 4
    up, down = chip_sum(early[:, n:]), halved(early[:, :n], rank, 0)
    gq, gk, gv = near_back(q, k, v, docs, gmerged, lmf, dd, 8, 8, nears, [early])
    far_k, far_v, *turned = far_back(k, v, docs, guests, [gq])
    back = [(level, exchanged(x, "seq", mask)) for (level, mask), x in zip(visits, turned)]
    to_near, own_part, keys_mine, keys_theirs, sums = keys_last(
        where, qkv_shards, (gk, gv, far_k, far_v), normed, [up, down])
    got = exchanged(to_near, "seq", 1)
    up, down = halved(up, rank, 1), chip_sum(down)
    keys = chip_sum(core_sum(keys_mine, keys_theirs))
    grad_tiles, late_mine, late_theirs = last(
        where, qkv_shards, gq, back, normed, inputs, gmid, vectors, small, gbias, own_part, got, sums, [up, down])
    up, down, keys = beyond(up, seq), beyond(down, seq), beyond(keys, seq)
    up, down = halved(up, rank, 0), halved(down, rank, 1)
    up, down = halved(up, rank, 2), halved(down, rank, 2)
    for bit in (1, 0, 2):
        keys = halved(keys, rank, bit)
    up, down = doubled(up, rank, 2), doubled(down, rank, 2)
    up, down = doubled(up, rank, 0), doubled(down, rank, 1)
    up, down = doubled(up, rank, 1), doubled(down, rank, 0)
    for bit in (2, 0, 1):
        keys = doubled(keys, rank, bit)
    late = direct(late_mine, late_theirs, seq).astype(f32)
    sum_up, sum_down, late_keys = [x[0].astype(f32) for x in (up, down, keys)]

    side_by_side = lambda a: a.reshape(-1, D // 4, D).swapaxes(0, 1).reshape(D // 4, -1)
    tiny = late[D // 4 : D // 4 + 16]
    mine = lax.dynamic_slice_in_dim(tiny[:8], part * cols, cols, 1)
    sum_bias = lax.dynamic_slice_in_dim(tiny[8:12], part, 1, 0).reshape(-1)
    return (
        encoded[None],
        grad_tiles[None],
        side_by_side(jnp.concatenate([late[: D // 4], late_keys], axis=0)), sum_down[FF_PART:], side_by_side(sum_up), sum_down[:FF_PART],
        mine[:2], mine[2:], sum_bias,
    )


def solution(mesh):
    tokens, rows, cols = P("fsdp", "seq", None), P("fsdp", None), P(None, "fsdp")
    return jax.shard_map(
        local,
        mesh=mesh,
        in_specs=(tokens, P("fsdp", "seq"), tokens, rows, rows, rows, rows, cols, cols, P("fsdp")),
        out_specs=(tokens, tokens, rows, rows, rows, rows, cols, cols, P("fsdp")),
        check_vma=False,
    )
```

```python
import functools
import math

import jax
import jax.numpy as jnp
import ml_dtypes
import numpy as np
from jax import lax
from jax.experimental import pallas as pl
from jax.experimental.pallas import tpu as pltpu
from jax.sharding import PartitionSpec as P

HEADS = 16
HD = 48
D = HEADS * HD
SEG_BASE = 1024
BRANCHES = 5
T = 512
RES = 16
EPS = 1e-05
BIG = 2.0**100
SCALE = HD**-0.5
VMEM = 56 << 20
ORDER = np.array([int(f"{c:04b}"[::-1], 2) for c in range(RES)])
bf16, f32 = jnp.bfloat16, jnp.float32

VM = pl.BlockSpec(memory_space=pltpu.VMEM)
SM = pl.BlockSpec(memory_space=pltpu.SMEM)
HB = pl.BlockSpec(memory_space=pl.ANY)


def tdot(a, b):
    return lax.dot_general(a, b, (((0,), (0,)), ((), ())), preferred_element_type=f32)


def ndot(a, b):
    return lax.dot_general(a, b, (((1,), (0,)), ((), ())), preferred_element_type=f32)


def bdot(a, b):
    return lax.dot_general(a, b, (((1,), (1,)), ((), ())), preferred_element_type=f32)


def xdot(a, b):
    return lax.dot_general(a, b, (((0,), (1,)), ((), ())), preferred_element_type=f32)


def cost(us):
    return pl.CostEstimate(flops=int(us * 1e9), bytes_accessed=1000, transcendentals=0)


def kernel_call(body, in_specs, after=(), **kwargs):
    count = len(after)
    call = pl.pallas_call(
        (lambda *refs: body(*refs[count:])) if count else body,
        in_specs=[HB] * count + in_specs,
        compiler_params=pltpu.CompilerParams(vmem_limit_bytes=VMEM),
        **kwargs,
    )
    return functools.partial(call, *after)


def bit_reversed(h):
    return (h % 2) * 8 + (h // 2 % 2) * 4 + (h // 4 % 2) * 2 + h // 8


def split2(x):
    hi = x.astype(bf16)
    return hi, (x - hi.astype(f32)).astype(bf16)


def split3(x):
    a = x.astype(bf16).astype(f32)
    b = (x - a).astype(bf16).astype(f32)
    return a, b, x - a - b


def log_ratio(level):
    out = []
    for t in range(1, BRANCHES):
        c = math.log2((t + 1 - level) / (t - level)) if t > level else 0.0
        hi = float(np.asarray(c).astype(ml_dtypes.bfloat16))
        out.append((hi, float(np.asarray(c - hi).astype(ml_dtypes.bfloat16))))
    return out


def valuation(g, pos):
    c = pos >> 5
    hits = [((c >> n) == (g >> n)).astype(jnp.int32) for n in (3, 2, 1, 0)]
    return hits[0] + hits[1] + hits[2] + hits[3]


def query_side(g, q, docs, pos, level, lm=None):
    n = q.shape[1]
    hi, lo = split2(q.astype(f32) * (SCALE * math.log2(math.e)))
    row = lax.broadcasted_iota(jnp.int32, (32, n), 0)
    v = valuation(g, pos)
    f = jnp.where((row < 4) & (row == docs), -BIG, 0.0)
    for i, parts in enumerate(log_ratio(level)):
        for j, part in enumerate(parts):
            if part:
                f = jnp.where((row == 4 + 2 * i + j) & (v > i), part, f)
    if level >= 3:
        f = jnp.where(row == 12, -BIG, f)
    if level >= 4:
        f = jnp.where(row == 13, -BIG, f)
    if lm is not None:
        for r, part in enumerate(split3(lm)):
            f = jnp.where(row == 14 + r, -part, f)
    return jnp.concatenate([hi, lo, f.astype(bf16)], axis=0)


def key_side(g, k, docs):
    n = k.shape[1]
    pos = lax.broadcasted_iota(jnp.int32, (1, n), 1) & (T - 1)
    row = lax.broadcasted_iota(jnp.int32, (32, n), 0)
    v = valuation(g, pos)
    f = jnp.where((row < 4) & (row != docs), 1.0, 0.0)
    f = jnp.where((row >= 4) & (row < 12) & (v >= ((row - 2) >> 1)), 1.0, f)
    f = jnp.where((row == 12) & (v < 3), 1.0, f)
    f = jnp.where((row == 13) & (v < 4), 1.0, f)
    f = jnp.where((row >= 14) & (row < 17), 1.0, f)
    return jnp.concatenate([k, k, f.astype(bf16)], axis=0)


def ones_below(v, count):
    row = lax.broadcasted_iota(jnp.int32, (16, v.shape[1]), 0)
    return jnp.concatenate([v, jnp.where(row < count, 1.0, 0.0).astype(bf16)], axis=0)


def positions(first, n, width):
    return first + (lax.broadcasted_iota(jnp.int32, (1, n), 1) & (width - 1))


def attend(jobs):
    scores = [tdot(kf, qf) for kf, _, qf in jobs]
    tops = [jnp.max(s, axis=0, keepdims=True) for s in scores]
    weights = [jnp.exp2(s - m).astype(bf16) for s, m in zip(scores, tops)]
    outs = [ndot(v1, p) for (_, v1, _), p in zip(jobs, weights)]
    return [(o[:HD] * (1.0 / o[HD : HD + 1]), m + jnp.log2(o[HD : HD + 1])) for o, m in zip(outs, tops)]


def attend_back(jobs):
    weights = [jnp.exp2(tdot(kf, qf)) for kf, _, _, qf, _, _ in jobs]
    slopes = [tdot(v3, gf) for _, _, v3, _, _, gf in jobs]
    ds = [(p * dp).astype(bf16) for p, dp in zip(weights, slopes)]
    ps = [p.astype(bf16) for p in weights]
    return [(ndot(k, d), bdot(q, d), bdot(gf[:HD], p)) for (_, k, _, _, q, gf), d, p in zip(jobs, ds, ps)]


def gradient_side(grad, dd):
    row = lax.broadcasted_iota(jnp.int32, (16, grad.shape[1]), 0)
    f = jnp.zeros((16, grad.shape[1]), f32)
    for r, part in enumerate(split3(dd)):
        f = jnp.where(row == r, -part, f)
    return jnp.concatenate([grad, f.astype(bf16)], axis=0)


TILE = 256
TILES = [slice(at, at + TILE) for at in range(0, T, TILE)]


def head_of(ref, i, rows=HD):
    return ref[i * rows : (i + 1) * rows]


def near_kernel(q_ref, k_ref, v_ref, docs_ref, o_ref, lm_ref):
    docs = docs_ref[...]
    jobs = []
    for i in range(NEAR):
        g = pl.program_id(0) * NEAR + i
        kf = key_side(g, head_of(k_ref, i), docs)
        v1 = ones_below(head_of(v_ref, i), 1)
        q = head_of(q_ref, i)
        jobs += [(kf, v1, query_side(g, q[:, c], docs[:, c], positions(c.start, TILE, T), 0)) for c in TILES]
    done = attend(jobs)
    for i in range(NEAR):
        for c in TILES:
            o, lm = done.pop(0)
            o_ref[i * HD : (i + 1) * HD, c] = o
            lm_ref[i, :, c] = lm


def window(ref, g, level):
    w = T >> min(level, 2)
    at = pl.multiple_of((g >> (4 - min(level, 2))) * w, 128)
    return jnp.concatenate([ref[:, pl.ds(at, w)], ref[:, pl.ds(T + at, w)]], axis=1)


def guest_side(g, level, q, docs_ref, lm=None):
    width = T >> level
    block = g >> (4 - level)
    rows = docs_ref[...].astype(f32)
    pick = lax.broadcasted_iota(jnp.int32, rows.shape, 0) == block
    docs = jnp.sum(jnp.where(pick, rows, 0.0), axis=0, keepdims=True).astype(jnp.int32)
    return query_side(g, q, docs, positions(block * width, q.shape[1], width), level, lm)


def parcel(features, numbers, rows):
    parts = [p for row in numbers for p in split3(row)]
    rest = rows - FAR * HD - len(parts)
    stats = jnp.concatenate(parts + [jnp.zeros((rest, numbers[0].shape[1]), f32)], axis=0).astype(bf16)
    return jnp.concatenate(features + [stats], axis=0)


def number(block, i):
    rows = block[FAR * HD + 3 * i : FAR * HD + 3 * i + 3].astype(f32)
    return rows[0:1] + rows[1:2] + rows[2:3]


def far_kernel(levels, k_ref, v_ref, docs_ref, *refs):
    kf_ref = refs[-1]
    ins, outs = refs[: 2 * len(levels)], refs[2 * len(levels) : -1]
    jobs = []
    for i in range(FAR):
        g = pl.program_id(0) * FAR + i
        kf_ref[i] = key_side(g, head_of(k_ref, i), docs_ref[...])
        rows = pl.ds(i * HD, HD)
        for j, level in enumerate(levels):
            qf = guest_side(g, level, head_of(ins[2 * j], i), ins[2 * j + 1])
            jobs.append((window(kf_ref.at[i], g, level), ones_below(window(v_ref.at[rows], g, level), 1), qf))
    done = attend(jobs)
    for j, out in enumerate(outs):
        mine = done[j :: len(outs)]
        out[...] = parcel([o.astype(bf16) for o, _ in mine], [lm for _, lm in mine], BACK)


def near_back_kernel(first, q_ref, k_ref, v_ref, docs_ref, g_ref, lm_ref, dd_ref, *refs):
    gq_ref, gk_ref, gv_ref = refs[-3:]
    docs = docs_ref[...]
    jobs = []
    for i in range(NEAR):
        g = pl.program_id(0) * NEAR + i + first
        k, q, grad, lm, dd = head_of(k_ref, i), head_of(q_ref, i), head_of(g_ref, i), lm_ref[i], dd_ref[i]
        kf = key_side(g, k, docs)
        v3 = ones_below(head_of(v_ref, i), 3)
        for c in TILES:
            qf = query_side(g, q[:, c], docs[:, c], positions(c.start, TILE, T), 0, lm[:, c])
            jobs.append((kf, k, v3, qf, q[:, c], gradient_side(grad[:, c], dd[:, c])))
    done = attend_back(jobs)
    for i in range(NEAR):
        rows = slice(i * HD, (i + 1) * HD)
        mine = [done.pop(0) for _ in TILES]
        for c, (dq, _, _) in zip(TILES, mine):
            gq_ref[rows, c] = (dq * SCALE).astype(bf16)
        gk_ref[rows] = (sum(d[1] for d in mine) * SCALE).astype(bf16)
        gv_ref[rows] = sum(d[2] for d in mine).astype(bf16)


def far_back_kernel(levels, k_ref, v_ref, docs_ref, *refs):
    kf_ref, ak_ref, av_ref = refs[-3:]
    n = len(levels)
    ins, outs = refs[: 3 * n], refs[3 * n : -3]
    parcels = [ref[...] for ref in ins[2::3]]
    jobs = []
    for i in range(FAR):
        g = pl.program_id(0) * FAR + i
        kf_ref[i] = key_side(g, head_of(k_ref, i), docs_ref[...])
        rows = pl.ds(i * HD, HD)
        for j, level in enumerate(levels):
            q_ref, dq_ref = ins[3 * j : 3 * j + 2]
            q, grad = head_of(q_ref, i), head_of(parcels[j], i)
            qf = guest_side(g, level, q, dq_ref, number(parcels[j], 2 * i))
            gf = gradient_side(grad, number(parcels[j], 2 * i + 1))
            k, v = window(k_ref.at[rows], g, level), window(v_ref.at[rows], g, level)
            jobs.append((window(kf_ref.at[i], g, level), k, ones_below(v, 3), qf, q, gf))
    done = attend_back(jobs)
    ak_ref[...] = jnp.zeros_like(ak_ref)
    av_ref[...] = jnp.zeros_like(av_ref)
    for i in range(FAR):
        g = pl.program_id(0) * FAR + i
        rows = slice(i * HD, (i + 1) * HD)
        for j, level in enumerate(levels):
            dq, dk, dv = done.pop(0)
            outs[2 + j][rows] = (dq * SCALE).astype(bf16)
            w = T >> min(level, 2)
            at = (g >> (4 - min(level, 2))) * w
            for c in range(2):
                cols = pl.ds(pl.multiple_of(c * T + at, 128), w)
                ak_ref[rows, cols] += dk[:, c * w : (c + 1) * w]
                av_ref[rows, cols] += dv[:, c * w : (c + 1) * w]
    outs[0][...] = (ak_ref[...] * SCALE).astype(bf16)
    outs[1][...] = av_ref[...].astype(bf16)


NEAR, FAR = 2, 4
BACK, OUT = FAR * HD + 16, FAR * HD + 32


def head_rows(n, heads, first=0, rows=HD):
    return pl.BlockSpec((rows * heads, n), lambda i: (i + first // heads, 0))


def head_stats(n, heads, first=0):
    return pl.BlockSpec((heads, 1, n), lambda i: (i + first // heads, 0, 0))


def whole(*shape):
    return pl.BlockSpec(shape, lambda i: (0,) * len(shape))


def guest_docs(n):
    return pl.BlockSpec((16, n), lambda i: (D // 16, 0))


def shape_of(*dims, dtype=bf16):
    return jax.ShapeDtypeStruct(dims, dtype)


def attend_near(q, k, v, docs):
    r = lambda n: head_rows(n, NEAR)
    return kernel_call(
        near_kernel,
        grid=(HEADS // NEAR,),
        in_specs=[r(T), r(2 * T), r(2 * T), whole(1, 2 * T)],
        out_specs=[r(T), head_stats(T, NEAR)],
        out_shape=[shape_of(D, T, dtype=f32), shape_of(HEADS, 1, T, dtype=f32)],
        cost_estimate=cost(1),
        name="near",
    )(q, k, v, docs)


def attend_far(k, v, docs, guests, after):
    r = lambda n: head_rows(n, FAR)
    in_specs = [r(2 * T), r(2 * T), whole(1, 2 * T)]
    out_specs, out_shape, args = [], [], []
    for level, q in guests:
        n = q.shape[1]
        in_specs += [r(n), guest_docs(n)]
        out_specs.append(head_rows(n, 1, 0, BACK))
        out_shape.append(shape_of(BACK * HEADS // FAR, n))
        args += [q, q]
    return kernel_call(
        functools.partial(far_kernel, [v[0] for v in guests]),
        after=after,
        grid=(HEADS // FAR,),
        in_specs=in_specs,
        out_specs=out_specs,
        out_shape=out_shape,
        scratch_shapes=[pltpu.VMEM((FAR, 128, 2 * T), bf16)],
        cost_estimate=cost(1),
        name="far",
    )(k, v, docs, *args)


def near_back(q, k, v, docs, grads, lm, dd, first, count, rest=(), after=()):
    r = lambda n: head_rows(n, NEAR, first)
    return kernel_call(
        functools.partial(near_back_kernel, first),
        after=after,
        grid=(count // NEAR,),
        in_specs=[r(T), r(2 * T), r(2 * T), whole(1, 2 * T), r(T), head_stats(T, NEAR, first), head_stats(T, NEAR, first)] + [HB] * len(rest),
        out_specs=[r(T), r(2 * T), r(2 * T)],
        out_shape=[shape_of(D, n) for n in (T, 2 * T, 2 * T)],
        input_output_aliases={len(after) + 7 + i: i for i in range(len(rest))},
        cost_estimate=cost(1),
        name="near_back",
    )(q, k, v, docs, grads, lm, dd, *rest)


def far_back(k, v, docs, guests, after):
    r = lambda n: head_rows(n, FAR)
    in_specs = [r(2 * T), r(2 * T), whole(1, 2 * T)]
    out_specs, out_shape, args = [r(2 * T)] * 2, [shape_of(D, 2 * T)] * 2, []
    for level, q, grads in guests:
        n = q.shape[1]
        in_specs += [r(n), guest_docs(n), head_rows(n, 1, 0, OUT)]
        out_specs.append(r(n))
        out_shape.append(shape_of(D, n))
        args += [q, q, grads]
    return kernel_call(
        functools.partial(far_back_kernel, [v[0] for v in guests]),
        after=after,
        grid=(HEADS // FAR,),
        in_specs=in_specs,
        out_specs=out_specs,
        out_shape=out_shape,
        scratch_shapes=[pltpu.VMEM((FAR, 128, 2 * T), bf16), pltpu.VMEM((FAR * HD, 2 * T), f32), pltpu.VMEM((FAR * HD, 2 * T), f32)],
        cost_estimate=cost(1),
        name="far_back",
    )(k, v, docs, *args)


def permutation():
    p = lax.broadcasted_iota(jnp.int32, (T, T), 0)
    o = lax.broadcasted_iota(jnp.int32, (T, T), 1)
    return jnp.where(o == p % 32 * RES + bit_reversed(p // 32), 1.0, 0.0).astype(bf16)


def normalized(x):
    center = jnp.mean(x, axis=-1, keepdims=True)
    centered = x - center
    rstd = lax.rsqrt(jnp.mean(centered * centered, axis=-1, keepdims=True) + EPS)
    return centered * rstd, rstd


def norm_pullback(grad, xhat, rstd, gain):
    g = grad * gain
    gx = rstd * (g - jnp.mean(g, axis=-1, keepdims=True) - xhat * jnp.mean(g * xhat, axis=-1, keepdims=True))
    return gx, jnp.sum(grad * xhat, axis=0, keepdims=True), jnp.sum(grad, axis=0, keepdims=True)


def fetch(shards, buffer, sems, where_ref, rows):
    out = []
    for r, shard in enumerate(shards):
        at = pl.multiple_of(where_ref[r] * rows, rows)
        out.append(pltpu.make_async_copy(shard.at[pl.ds(0, rows)], buffer.at[pl.ds(at, rows)], sems.at[r]))
        out[-1].start()
    return out


def add_bias(values, row_ref, r):
    pick = jnp.where(lax.broadcasted_iota(jnp.int32, (16, values.shape[1]), 0) == r, 1.0, 0.0).astype(bf16)
    return values + tdot(row_ref, pick)


def block_lanes(g, level):
    at = g // (RES >> level) * (T >> level)
    return slice(at, at + (T >> level))


def head_slice(g):
    return slice(g * HD, (g + 1) * HD)


def project_kernel(levels, where_ref, w0, w1, w2, w3, vec_ref, bias_ref, docs_ref, x0_ref, x1_ref, *refs):
    q_ref, k_ref, v_ref, n_ref, in_ref, dout_ref = refs[:6]
    visit_refs = refs[6 : 5 + levels]
    w_ref, wt_ref, sems = refs[5 + levels :]
    copies = fetch((w0, w1, w2, w3), w_ref, sems, where_ref, D // 4)
    perm = permutation()
    gain, shift = vec_ref[0:1], vec_ref[2:3]

    def norm(x):
        xhat, _ = normalized(x.astype(f32))
        return ndot(perm, (xhat * gain + shift).astype(bf16)).astype(bf16)

    in_ref[...] = ndot(perm, x0_ref[...]).astype(bf16)
    n_ref[:T] = norm(x0_ref[...])
    n_ref[T:] = norm(x1_ref[:T])
    own_docs = bdot(jnp.broadcast_to(docs_ref[...].astype(f32), (8, T)).astype(bf16), perm)[0:1]
    near_docs = bdot(x1_ref[T:, :T], perm)[0:1]
    dout_ref[...] = jnp.concatenate([own_docs, near_docs], axis=1).astype(jnp.int32)
    for c in copies:
        c.wait()
    for part in range(3):
        wt = w_ref[:, part * D : (part + 1) * D].T
        for g in range(HEADS):
            h = int(ORDER[g])
            wt_ref[part * D + g * HD : part * D + (g + 1) * HD, :] = wt[head_slice(h)]
    n = n_ref[...]
    q_ref[...] = add_bias(bdot(wt_ref[:D, :], n_ref[:T]), bias_ref[...], 0).astype(bf16)
    for level in range(1, levels):
        width = T >> level
        visit = visit_refs[level - 1]
        for g in range(HEADS):
            visit[head_slice(g), :] = q_ref[head_slice(g), block_lanes(g, level)]
        rows = [own_docs[:, b * width : (b + 1) * width] for b in range(1 << level)]
        if level < 4:
            rows.append(jnp.zeros((16 - len(rows), width), f32))
        visit[D:, :] = jnp.concatenate(rows, axis=0).astype(bf16)
    k_ref[...] = bdot(wt_ref[D : 2 * D, :], n).astype(bf16)
    v_ref[...] = add_bias(bdot(wt_ref[2 * D :, :], n), bias_ref[...], 1).astype(bf16)


def project(levels, where, shards, vectors, biases, docs, tile, tile_near):
    return kernel_call(
        functools.partial(project_kernel, levels),
        in_specs=[SM] + [HB] * 4 + [VM] * 5,
        out_specs=[VM] * (5 + levels),
        out_shape=[shape_of(D, T), shape_of(D, 2 * T), shape_of(D, 2 * T), shape_of(2 * T, D), shape_of(T, D), shape_of(1, 2 * T, dtype=jnp.int32)]
        + [shape_of(D + 16, T >> level) for level in range(1, levels)],
        scratch_shapes=[pltpu.VMEM((D, 3 * D), bf16), pltpu.VMEM((3 * D, D), bf16), pltpu.SemaphoreType.DMA((4,))],
        cost_estimate=cost(1),
        name="project",
    )(where, *shards, vectors, biases, docs, tile, tile_near)


ERF_TOP = (0.00022905065861350646, 0.0034082910107109506, 0.050955695062380861, 0.18520832239976145, 1.128379143519084)
ERF_BOTTOM = (-1.1791602954361697e-7, 0.000023547966471313185, 0.0010179625278914885, 0.014070470171167667, 0.11098505178285362, 0.49746925110067538, 1.0)


def erf(x):
    x = jnp.clip(x, -3.7439211627767994, 3.7439211627767994)
    y = x * x
    top, bottom = ERF_TOP[0], ERF_BOTTOM[0]
    for c in ERF_TOP[1:]:
        top = top * y + c
    for c in ERF_BOTTOM[1:]:
        bottom = bottom * y + c
    return x * top / bottom


FF_PART = 768
FF_ROWS = 2 * FF_PART + D // 4


def merge_heads(o_ref, lm_ref, back, merged_ref, lmf_ref):
    for g in range(HEADS):
        base = lm_ref[g]
        parts, top = [], base
        blocks = [head_of(ref, g // FAR, BACK) for _, ref in back]
        for (level, _), block in zip(back, blocks):
            cols = block_lanes(g, level)
            rest = [jnp.full((1, n), -BIG, f32) for n in (cols.start, T - cols.stop)]
            parts.append(jnp.concatenate([x for x in (rest[0], number(block, g % FAR), rest[1]) if x.shape[1]], axis=1))
            top = jnp.maximum(top, parts[-1])
        weights = [jnp.exp2(x - top) for x in [base] + parts]
        total = sum(weights)
        scale = 1.0 / total
        out = o_ref[head_slice(g), :] * (weights[0] * scale)
        for (level, _), block, w in zip(back, blocks, weights[1:]):
            cols = block_lanes(g, level)
            add = head_of(block, g % FAR).astype(f32) * (w * scale)[:, cols]
            rest = [jnp.zeros((HD, n), f32) for n in (cols.start, T - cols.stop)]
            out = out + jnp.concatenate([x for x in (rest[0], add, rest[1]) if x.shape[1]], axis=1)
        merged_ref[head_slice(int(ORDER[g])), :] = out
        lmf_ref[g] = top + jnp.log2(total)


def middle_kernel(levels, back_levels, where_ref, *refs):
    shards, refs = refs[:4], refs[4:]
    o_ref, lm_ref, in_ref, cot_ref, vec_ref, hb_ref = refs[:6]
    n = len(back_levels)
    back = list(zip(back_levels, refs[6 : 6 + n]))
    refs = refs[6 + n :]
    enc_ref, mine_out, theirs_out, gm_ref, dd_ref, lmf_ref, gmid_ref, small_ref, gbias_ref = refs[:9]
    grad_out = lambda r, at, rows: (mine_out, theirs_out)[r % 2].at[r // 2, pl.ds(at, rows)]
    visit_refs, refs = refs[9 : 8 + levels], refs[8 + levels :]
    wo_ref, wu_ref, wd_ref, gd_ref, gu_ref, act_ref, merged_ref, y_ref, gn_ref, gy_ref, n2_ref, sems, osems = refs
    out_copies = fetch(shards, wo_ref, sems.at[0], where_ref, D // 4)
    up_copies, down_copies = [], []
    for r, shard in enumerate(shards):
        rows = pl.ds(pl.multiple_of(where_ref[r] * (D // 4), D // 4), D // 4)
        for c in range(4):
            dst = wu_ref.at[rows, pl.ds(c * FF_PART, FF_PART)]
            up_copies.append(pltpu.make_async_copy(shard.at[pl.ds((1 + c) * (D // 4), D // 4)], dst, sems.at[1 + c, r]))
            up_copies[-1].start()
    for r, shard in enumerate(shards):
        down_copies.append(pltpu.make_async_copy(shard.at[pl.ds(5 * (D // 4), FF_PART)], wd_ref.at[r], sems.at[5, r]))
        down_copies[-1].start()
    perm = permutation()
    gy_ref[...] = ndot(perm, cot_ref[...]).astype(bf16)
    merge_heads(o_ref, lm_ref, back, merged_ref, lmf_ref)
    merged = merged_ref[...].astype(bf16)
    for c in out_copies:
        c.wait()
    middle = in_ref[...].astype(f32) + tdot(merged, wo_ref[...]) + vec_ref[5:6]
    xhat, rstd = normalized(middle)
    n2_ref[...] = (xhat * vec_ref[1:2] + vec_ref[6:7]).astype(bf16)
    y_ref[...] = middle + vec_ref[7:8]
    gn_ref[...] = jnp.zeros_like(gn_ref)
    for c in up_copies:
        c.wait()
    down_parts = []
    for r in range(4):
        at = pl.multiple_of(where_ref[r] * FF_PART, FF_PART)
        cols = pl.ds(at, FF_PART)
        down_copies[r].wait()
        n2, gy = n2_ref[...], gy_ref[...]
        hidden = ndot(n2, wu_ref[:, cols]) + hb_ref[:, cols]
        phi = 0.5 + 0.5 * erf(hidden * 0.5**0.5)
        slope = phi + hidden * (jnp.exp(hidden * hidden * -0.5) * (2 * math.pi) ** -0.5)
        active = (hidden * phi).astype(bf16)
        y_ref[...] += ndot(active, wd_ref[r])
        gd_ref[r] = tdot(active, gy).astype(bf16)
        down_parts.append(pltpu.make_async_copy(gd_ref.at[r], grad_out(r, 0, FF_PART), osems.at[r]))
        down_parts[-1].start()
        gh = (slope * bdot(gy, wd_ref[r])).astype(bf16)
        gbias_ref[:, cols] = jnp.sum(gh.astype(f32), axis=0, keepdims=True)
        gu_ref[:, cols] = tdot(n2, gh).astype(bf16)
        gn_ref[...] += bdot(gh, wu_ref[:, cols])
    up_parts = []
    for r in range(4):
        at = pl.multiple_of(where_ref[r] * (D // 4), D // 4)
        for c in range(4):
            src = gu_ref.at[pl.ds(at, D // 4), pl.ds(c * FF_PART, FF_PART)]
            up_parts.append(pltpu.make_async_copy(src, grad_out(r, FF_PART + (1 + c) * (D // 4), D // 4), osems.at[8 + 4 * r + c]))
            up_parts[-1].start()
    enc_ref[...] = tdot(perm, y_ref[...].astype(bf16)).astype(bf16)
    gy = gy_ref[...].astype(f32)
    middle = in_ref[...].astype(f32) + tdot(merged, wo_ref[...]) + vec_ref[5:6]
    xhat, rstd = normalized(middle)
    gx, ggain, gshift = norm_pullback(gn_ref[...], xhat, rstd, vec_ref[1:2])
    gmid = gy + gx
    gmid_ref[...] = gmid
    gatt = gmid.astype(bf16)
    act_ref[...] = ndot(merged, gatt).astype(bf16)
    for r in range(4):
        at = pl.multiple_of(where_ref[r] * (D // 4), D // 4)
        down_parts.append(pltpu.make_async_copy(act_ref.at[pl.ds(at, D // 4)], grad_out(r, FF_PART, D // 4), osems.at[4 + r]))
        down_parts[-1].start()
    gm = bdot(wo_ref[...], gatt)
    prod = gm * merged_ref[...]
    gm = gm.astype(bf16)
    dds = [None] * HEADS
    for g in range(HEADS):
        h = head_slice(int(ORDER[g]))
        gm_ref[head_slice(g), :] = gm[h]
        dds[g] = jnp.sum(prod[h], axis=0, keepdims=True)
        dd_ref[g] = dds[g]
    for level in range(1, levels):
        for first in range(0, HEADS, FAR):
            features, numbers = [], []
            for g in range(first, first + FAR):
                cols = block_lanes(g, level)
                features.append(gm[head_slice(int(ORDER[g])), cols])
                numbers += [lmf_ref[g][:, cols], dds[g][:, cols]]
            at = first // FAR * OUT
            visit_refs[level - 1][at : at + OUT, :] = parcel(features, numbers, OUT)
    zero = jnp.zeros((4, D), f32)
    small_ref[...] = jnp.concatenate(
        [ggain, jnp.sum(gatt.astype(f32), axis=0, keepdims=True), gshift, jnp.sum(gy, axis=0, keepdims=True), zero], axis=0)
    for c in down_parts + up_parts:
        c.wait()


def middle(levels, where, shards, o, lm, back, inputs, cotangent, vectors, bias, after):
    s = shape_of
    ff = bias.shape[1]
    visits = [s(OUT * HEADS // FAR, T >> level) for level in range(1, levels)]
    return kernel_call(
        functools.partial(middle_kernel, levels, [b[0] for b in back]),
        after=after,
        in_specs=[SM] + [HB] * 4 + [VM] * (6 + len(back)),
        out_specs=[VM] + [HB] * 2 + [VM] * (6 + len(visits)),
        out_shape=[
            s(T, D), s(2, FF_ROWS, D), s(2, FF_ROWS, D),
            s(D, T), s(HEADS, 1, T, dtype=f32), s(HEADS, 1, T, dtype=f32), s(T, D, dtype=f32), s(8, D, dtype=f32), s(1, ff, dtype=f32),
        ] + visits,
        scratch_shapes=[
            pltpu.VMEM((D, D), bf16), pltpu.VMEM((D, ff), bf16), pltpu.VMEM((4, FF_PART, D), bf16),
            pltpu.VMEM((4, FF_PART, D), bf16), pltpu.VMEM((D, ff), bf16), pltpu.VMEM((D, D), bf16), pltpu.VMEM((D, T), f32),
            pltpu.VMEM((T, D), f32), pltpu.VMEM((T, D), f32), pltpu.VMEM((T, D), bf16), pltpu.VMEM((T, D), bf16),
            pltpu.SemaphoreType.DMA((6, 4)), pltpu.SemaphoreType.DMA((24,)),
        ],
        cost_estimate=cost(1),
        name="middle",
    )(where, *shards, o, lm, inputs, cotangent, vectors, bias, *[b[1] for b in back])


def natural(refs):
    rows = []
    for h in range(HEADS):
        g = head_slice(int(ORDER[h]))
        rows.append(sum(ref[g, :].astype(f32) for ref in refs).astype(bf16))
    return jnp.concatenate(rows, axis=0)


def to_blocks(where_ref, src_ref, out_refs, parts):
    rows = D // 4
    for r in range(4):
        at = pl.multiple_of(where_ref[r] * rows, rows)
        for part in range(parts):
            out_refs[r % 2][r // 2, part * rows : (part + 1) * rows, :] = src_ref[pl.ds(at, rows), part * D : (part + 1) * D]


def keys_kernel(where_ref, w0, w1, w2, w3, nk_ref, nv_ref, fk_ref, fv_ref, n_ref, vec_ref,
                send_ref, own_ref, mine_ref, theirs_ref, sums_ref, w_ref, gp_ref, gw_ref, sems):
    copies = fetch((w0, w1, w2, w3), w_ref, sems, where_ref, D // 4)
    gp_ref[:D] = natural((nk_ref, fk_ref))
    gp_ref[D:] = natural((nv_ref, fv_ref))
    for c in copies:
        c.wait()
    send = xdot(gp_ref[:, T:], w_ref[:, D:])
    send_ref[...] = send.astype(bf16)
    gw_ref[...] = xdot(n_ref[...], gp_ref[...]).astype(bf16)
    to_blocks(where_ref, gw_ref, (mine_ref, theirs_ref), 2)
    own_ref[...] = xdot(gp_ref[:, :T], w_ref[:, D:])
    xhat = (n_ref[T:].astype(f32) - vec_ref[2:3]) / vec_ref[0:1]
    rows = [bdot(jnp.ones((16, 2 * T), bf16), gp_ref[D:, :])[0:1]]
    rows += [jnp.sum(send * xhat, axis=0, keepdims=True), jnp.sum(send, axis=0, keepdims=True), jnp.zeros((5, D), f32)]
    sums_ref[...] = jnp.concatenate(rows, axis=0)


def keys_last(where, shards, grads, normed, vectors, after):
    s = shape_of
    return kernel_call(
        keys_kernel,
        after=after,
        in_specs=[SM] + [HB] * 4 + [VM] * 6,
        out_specs=[VM] * 5,
        out_shape=[s(T, D), s(T, D, dtype=f32), s(2, D // 2, D), s(2, D // 2, D), s(8, D, dtype=f32)],
        scratch_shapes=[pltpu.VMEM((D, 3 * D), bf16), pltpu.VMEM((2 * D, 2 * T), bf16), pltpu.VMEM((D, 2 * D), bf16), pltpu.SemaphoreType.DMA((4,))],
        cost_estimate=cost(1),
        name="keys_last",
    )(where, *shards, *grads, normed, vectors)


LAST_ROWS = 256


def queries_kernel(back_levels, where_ref, w0, w1, w2, w3, gq_ref, *refs):
    back = list(zip(back_levels, refs))
    n_ref, in_ref, vec_ref, small_ref, gbias_ref, own_ref, sums_ref = refs[len(back) : len(back) + 7]
    grad_ref, mine_ref, theirs_ref, w_ref, gp_ref, gw_ref, sems = refs[len(back) + 7 :]
    copies = fetch((w0, w1, w2, w3), w_ref, sems, where_ref, D // 4)
    for g in range(HEADS):
        rows = head_slice(g)
        total = gq_ref[rows, :].astype(f32)
        for level, ref in back:
            cols = block_lanes(g, level)
            rest = [jnp.zeros((HD, n), f32) for n in (cols.start, T - cols.stop)]
            total = total + jnp.concatenate([x for x in (rest[0], ref[rows, :].astype(f32), rest[1]) if x.shape[1]], axis=1)
        gp_ref[head_slice(int(ORDER[g])), :] = total.astype(bf16)
    gw_ref[...] = xdot(n_ref[:T], gp_ref[...]).astype(bf16)
    to_blocks(where_ref, gw_ref, (mine_ref, theirs_ref), 1)
    sums = bdot(jnp.ones((16, T), bf16), gp_ref[...])
    xhat, _ = normalized(in_ref[...].astype(f32))
    for c in copies:
        c.wait()
    grad = xdot(gp_ref[...], w_ref[:, :D]) + own_ref[...]
    grad_ref[...] = grad
    ggain = jnp.sum(grad * xhat, axis=0, keepdims=True) + sums_ref[1:2]
    gshift = jnp.sum(grad, axis=0, keepdims=True) + sums_ref[2:3]
    rows = [ggain, small_ref[0:1], gshift, sums[0:1], sums_ref[0:1], small_ref[1:4]]
    rows += [gbias_ref[:, i * D : (i + 1) * D] for i in range(4)]
    rows += [jnp.zeros((4, D), f32)]
    small = jnp.concatenate(rows, axis=0).astype(bf16)
    for out in (mine_ref, theirs_ref):
        for r in range(2):
            out[r, D // 4 : D // 4 + 16, :] = small
            out[r, D // 4 + 16 :, :] = jnp.zeros((LAST_ROWS - D // 4 - 16, D), bf16)


def queries_last(where, shards, gq, back, normed, inputs, vectors, small, gbias, own, sums, after):
    return kernel_call(
        functools.partial(queries_kernel, [b[0] for b in back]),
        after=after,
        in_specs=[SM] + [HB] * 4 + [VM] * (8 + len(back)),
        out_specs=[VM] * 3,
        out_shape=[shape_of(T, D, dtype=f32), shape_of(2, LAST_ROWS, D), shape_of(2, LAST_ROWS, D)],
        scratch_shapes=[pltpu.VMEM((D, 3 * D), bf16), pltpu.VMEM((D, T), bf16), pltpu.VMEM((D, D), bf16), pltpu.SemaphoreType.DMA((4,))],
        cost_estimate=cost(1),
        name="queries_last",
    )(where, *shards, gq, *[b[1] for b in back], normed, inputs, vectors, small, gbias, own, sums)


def last_kernel(grad_ref, in_ref, gmid_ref, vec_ref, got_ref, gt_ref):
    xhat, rstd = normalized(in_ref[...].astype(f32))
    gx, _, _ = norm_pullback(grad_ref[...] + got_ref[...].astype(f32), xhat, rstd, vec_ref[0:1])
    gt_ref[...] = tdot(permutation(), (gmid_ref[...] + gx).astype(bf16)).astype(bf16)


def last(grad, inputs, gmid, vectors, got, after):
    return kernel_call(
        last_kernel,
        after=after,
        in_specs=[VM] * 5,
        out_specs=VM,
        out_shape=shape_of(T, D),
        cost_estimate=cost(1),
        name="last",
    )(grad, inputs, gmid, vectors, got)


def gate_kernel(*refs):
    refs[-1][...] = jnp.zeros_like(refs[-1])


def gate(arrays, us):
    return kernel_call(
        gate_kernel,
        in_specs=[HB] * len(arrays),
        out_specs=VM,
        out_shape=shape_of(8, 128, dtype=f32),
        cost_estimate=cost(us),
        name="gate",
    )(*arrays)


def exchanged(x, axis, mask):
    return lax.ppermute(x, axis, [(i, i ^ mask) for i in range(lax.axis_size(axis))])


def added(a, b):
    return (a.astype(f32) + b.astype(f32)).astype(bf16)


def behind(x, other):
    return lax.optimization_barrier((x, other))[0]


class Chain:
    def __init__(self, line, steps):
        self.line, self.steps = line, list(steps)

    def begin(self, value, theirs=None):
        self.value = value
        self.launch(theirs)
        return self

    def launch(self, theirs=None):
        x, line = self.value, self.line
        if not self.steps:
            return
        step = self.steps[0]
        if step == "c":
            self.kept, self.got = x, exchanged(theirs, "fsdp", 1)
        elif step == "x":
            self.kept, self.got = x[:1], exchanged(x[1:], "fsdp", 2)
        elif step == "a":
            self.got = lax.all_to_all(x.reshape(line.seq, -1, D), "seq", 0, 0)
        elif step == "g":
            self.got = lax.all_to_all(jnp.broadcast_to(x, (line.seq,) + x.shape[1:]), "seq", 0, 0)
        elif step in ("F0", "F1", "F2"):
            self.kept, self.got = x, exchanged(x, "seq", 1 << int(step[1]))
        elif isinstance(step, int):
            half = x.shape[1] // 2
            mine = line.rank >> step & 1
            self.kept = lax.dynamic_slice_in_dim(x, mine * half, half, 1)
            self.got = exchanged(lax.dynamic_slice_in_dim(x, (1 - mine) * half, half, 1), "seq", 1 << step)
        else:
            self.got = exchanged(x, "seq", 1 << int(step))

    def advance(self):
        step, got = self.steps.pop(0), behind(self.got, self.line.token)
        if step == "a":
            out = jnp.sum(got.astype(f32), axis=0, keepdims=True).astype(bf16)
        elif step == "g":
            out = got.reshape(1, -1, D)
        elif isinstance(step, str) and step.isdigit():
            x, low = self.value, (self.line.rank >> int(step) & 1) == 0
            out = jnp.concatenate([jnp.where(low, x, got), jnp.where(low, got, x)], axis=1)
        else:
            out = added(self.kept, got)
            if step == "x":
                for bit in range(3, self.line.seq.bit_length() - 1):
                    if "a" not in self.steps:
                        out = added(out, exchanged(out, "seq", 1 << bit))
        self.value = self.line.token = out
        self.launch()


class Line:
    def __init__(self, rank, seq, token):
        self.rank, self.seq, self.token = rank, seq, token


def local(tiles, documents, cotangent, w_qkv, w_out, w_up, w_down, gains, shifts, hidden_bias):
    seq = lax.axis_size("seq")
    rank = lax.axis_index("seq")
    part = lax.axis_index("fsdp")
    levels = min(BRANCHES, (seq * T // SEG_BASE).bit_length())
    where = jnp.stack([part ^ r for r in range(4)]).astype(jnp.int32)
    visits = [(level, (1 << level) + 2 * c) for level in range(1, levels) for c in range(1 << level - 1)]
    cols = gains.shape[1]

    packed = jnp.concatenate([gains, shifts, hidden_bias.reshape(-1, cols)], axis=0).reshape(1, -1)
    w_ext = jnp.concatenate([w_qkv, jnp.pad(packed, ((0, 7), (0, 0)))], axis=0)
    qkv_far = exchanged(w_ext, "fsdp", 2)
    tile = tiles[0]
    docs_row = jnp.pad(documents.astype(bf16), ((0, 7), (0, D - T)))
    tile_near = exchanged(jnp.concatenate([tile, docs_row], axis=0), "seq", 1)
    stacked_up = w_up.reshape(cols, -1, D).swapaxes(0, 1).reshape(-1, D)
    w_ff = jnp.concatenate([w_out, stacked_up, w_down], axis=0)
    ff_far = exchanged(w_ff, "fsdp", 2)
    qkv_near = exchanged(w_ext, "fsdp", 1)
    qkv_shards = (w_ext, qkv_near, qkv_far, exchanged(behind(qkv_far, tile_near), "fsdp", 1))
    ff_near = exchanged(w_ff, "fsdp", 1)

    stacked = jnp.stack([w[cols].reshape(-1, cols) for w in qkv_shards])
    in_order = jnp.stack([lax.dynamic_index_in_dim(stacked, part ^ s, 0, keepdims=False) for s in range(4)])
    rows = in_order[:, :8].transpose(1, 0, 2).reshape(8, D)
    vectors = rows.astype(f32)
    bias_row = in_order[:, 8:].reshape(1, -1).astype(f32)
    by_head = rows[3:5].reshape(2, 2, 2, 2, 2, HD).transpose(0, 4, 3, 2, 1, 5).reshape(2, D)
    biases = jnp.concatenate([by_head, jnp.zeros((14, D), bf16)], axis=0)

    q, k, v, normed, inputs, docs, *queries = project(levels, where, qkv_shards, vectors, biases, documents, tile, tile_near)
    guests = [(level, exchanged(queries[level - 1], "seq", mask)) for level, mask in visits]
    o, lm = attend_near(q, k, v, docs)
    partial = attend_far(k, v, docs, guests, [lm])
    back = [(level, exchanged(x, "seq", mask)) for (level, mask), x in zip(visits, partial)]
    returned = gate([x for _, x in back], 8)
    shards = (w_ff, ff_near, ff_far, exchanged(behind(ff_far, returned), "fsdp", 1))

    encoded, early_mine, early_theirs, gmerged, dd, lmf, gmid, small, gbias, *send = middle(
        levels, where, shards, o, lm, back, inputs, cotangent[0], vectors, bias_row, [returned])
    early_theirs = exchanged(early_theirs, "fsdp", 1)
    guests = [guest + (exchanged(send[level - 1], "seq", mask),) for guest, (level, mask) in zip(guests, visits)]
    arrived = gate([guest[2] for guest in guests], 8)
    nears = near_back(q, k, v, docs, gmerged, lmf, dd, 0, 4)
    early = added(early_mine, behind(early_theirs, nears[0]))
    n = FF_PART + D // 4
    line = Line(rank, seq, early)
    up = Chain(line, ["x", 1, 0, 2, "2", "0", "1"]).begin(early[:, n:])
    down = Chain(line, [0, "x", 1, 2, "2", "1", "0"]).begin(early[:, :n])
    keys = Chain(line, ["c", "x", 0, 1, 2, "2", "1", "0"])
    late = Chain(line, ["c", "x", "a", "g"])
    gq, gk, gv = near_back(q, k, v, docs, gmerged, lmf, dd, 4, 12, nears, [early])
    far_k, far_v, *turned = far_back(k, v, docs, guests, [gq, arrived])
    back = [(level, exchanged(x, "seq", mask)) for (level, mask), x in zip(visits, turned)]
    returned = gate([x for _, x in back], 30)

    line.token = far_k
    up.advance()
    down.advance()
    to_near, own_part, keys_mine, keys_theirs, sums = keys_last(
        where, qkv_shards, (gk, gv, far_k, far_v), normed, vectors, [line.token])
    got = exchanged(to_near, "seq", 1)
    keys.begin(keys_mine, keys_theirs)
    grad, late_mine, late_theirs = queries_last(
        where, qkv_shards, gq, back, normed, inputs, vectors, small, gbias, own_part, sums, [returned])
    late.begin(late_mine, late_theirs)
    line.token = late_mine
    for chain in (keys, up, late, down, up, late, keys, down, up, None, keys, down, up, late, keys, down, up, keys, down, keys, up, keys, late, down, keys):
        if chain is None:
            grad_tiles = line.token = last(grad, inputs, gmid, vectors, got, [line.token])
        else:
            chain.advance()
    sum_up, sum_down, late_keys, late = [c.value[0].astype(f32) for c in (up, down, keys, late)]

    side_by_side = lambda a: a.reshape(-1, D // 4, D).swapaxes(0, 1).reshape(D // 4, -1)
    tiny = late[D // 4 : D // 4 + 16]
    mine = lax.dynamic_slice_in_dim(tiny[:8], part * cols, cols, 1)
    sum_bias = lax.dynamic_slice_in_dim(tiny[8:12], part, 1, 0).reshape(-1)
    return (
        encoded[None],
        grad_tiles[None],
        side_by_side(jnp.concatenate([late[: D // 4], late_keys], axis=0)), sum_down[FF_PART:], side_by_side(sum_up), sum_down[:FF_PART],
        mine[:2], mine[2:], sum_bias,
    )


def solution(mesh):
    tokens, rows, cols = P("fsdp", "seq", None), P("fsdp", None), P(None, "fsdp")
    return jax.shard_map(
        local,
        mesh=mesh,
        in_specs=(tokens, P("fsdp", "seq"), tokens, rows, rows, rows, rows, cols, cols, P("fsdp")),
        out_specs=(tokens, tokens, rows, rows, rows, rows, cols, cols, P("fsdp")),
        check_vma=False,
    )
```

```python
import functools
import math

import jax
import jax.numpy as jnp
import ml_dtypes
import numpy as np
from jax import lax
from jax.experimental import pallas as pl
from jax.experimental.pallas import tpu as pltpu
from jax.sharding import PartitionSpec as P

HEADS = 16
HD = 48
D = HEADS * HD
SEG_BASE = 1024
BRANCHES = 5
T = 512
RES = 16
EPS = 1e-05
BIG = 2.0**100
SCALE = HD**-0.5
VMEM = 56 << 20
ORDER = np.array([int(f"{c:04b}"[::-1], 2) for c in range(RES)])
bf16, f32 = jnp.bfloat16, jnp.float32

VM = pl.BlockSpec(memory_space=pltpu.VMEM)
SM = pl.BlockSpec(memory_space=pltpu.SMEM)
HB = pl.BlockSpec(memory_space=pl.ANY)


def tdot(a, b):
    return lax.dot_general(a, b, (((0,), (0,)), ((), ())), preferred_element_type=f32)


def ndot(a, b):
    return lax.dot_general(a, b, (((1,), (0,)), ((), ())), preferred_element_type=f32)


def bdot(a, b):
    return lax.dot_general(a, b, (((1,), (1,)), ((), ())), preferred_element_type=f32)


def xdot(a, b):
    return lax.dot_general(a, b, (((0,), (1,)), ((), ())), preferred_element_type=f32)


def cost(us):
    return pl.CostEstimate(flops=int(us * 1e9), bytes_accessed=1000, transcendentals=0)


def kernel_call(body, in_specs, after=(), **kwargs):
    count = len(after)
    call = pl.pallas_call(
        (lambda *refs: body(*refs[count:])) if count else body,
        in_specs=[HB] * count + in_specs,
        compiler_params=pltpu.CompilerParams(vmem_limit_bytes=VMEM),
        **kwargs,
    )
    return functools.partial(call, *after)


def bit_reversed(h):
    return (h % 2) * 8 + (h // 2 % 2) * 4 + (h // 4 % 2) * 2 + h // 8


def split2(x):
    hi = x.astype(bf16)
    return hi, (x - hi.astype(f32)).astype(bf16)


def split3(x):
    a = x.astype(bf16).astype(f32)
    b = (x - a).astype(bf16).astype(f32)
    return a, b, x - a - b


def log_ratio(level):
    out = []
    for t in range(1, BRANCHES):
        c = math.log2((t + 1 - level) / (t - level)) if t > level else 0.0
        hi = float(np.asarray(c).astype(ml_dtypes.bfloat16))
        out.append((hi, float(np.asarray(c - hi).astype(ml_dtypes.bfloat16))))
    return out


def valuation(g, pos):
    c = pos >> 5
    hits = [((c >> n) == (g >> n)).astype(jnp.int32) for n in (3, 2, 1, 0)]
    return hits[0] + hits[1] + hits[2] + hits[3]


def query_side(g, q, docs, pos, level, lm=None):
    n = q.shape[1]
    hi, lo = split2(q.astype(f32) * (SCALE * math.log2(math.e)))
    row = lax.broadcasted_iota(jnp.int32, (32, n), 0)
    v = valuation(g, pos)
    f = jnp.where((row < 4) & (row == docs), -BIG, 0.0)
    for i, parts in enumerate(log_ratio(level)):
        for j, part in enumerate(parts):
            if part:
                f = jnp.where((row == 4 + 2 * i + j) & (v > i), part, f)
    if level >= 3:
        f = jnp.where(row == 12, -BIG, f)
    if level >= 4:
        f = jnp.where(row == 13, -BIG, f)
    if lm is not None:
        for r, part in enumerate(split3(lm)):
            f = jnp.where(row == 14 + r, -part, f)
    return jnp.concatenate([hi, lo, f.astype(bf16)], axis=0)


def key_side(g, k, docs):
    n = k.shape[1]
    pos = lax.broadcasted_iota(jnp.int32, (1, n), 1) & (T - 1)
    row = lax.broadcasted_iota(jnp.int32, (32, n), 0)
    v = valuation(g, pos)
    f = jnp.where((row < 4) & (row != docs), 1.0, 0.0)
    f = jnp.where((row >= 4) & (row < 12) & (v >= ((row - 2) >> 1)), 1.0, f)
    f = jnp.where((row == 12) & (v < 3), 1.0, f)
    f = jnp.where((row == 13) & (v < 4), 1.0, f)
    f = jnp.where((row >= 14) & (row < 17), 1.0, f)
    return jnp.concatenate([k, k, f.astype(bf16)], axis=0)


def ones_below(v, count):
    row = lax.broadcasted_iota(jnp.int32, (16, v.shape[1]), 0)
    return jnp.concatenate([v, jnp.where(row < count, 1.0, 0.0).astype(bf16)], axis=0)


def positions(first, n, width):
    return first + (lax.broadcasted_iota(jnp.int32, (1, n), 1) & (width - 1))


def attend(jobs):
    scores = [tdot(kf, qf) for kf, _, qf in jobs]
    tops = [jnp.max(s, axis=0, keepdims=True) for s in scores]
    weights = [jnp.exp2(s - m).astype(bf16) for s, m in zip(scores, tops)]
    outs = [ndot(v1, p) for (_, v1, _), p in zip(jobs, weights)]
    return [(o[:HD] * (1.0 / o[HD : HD + 1]), m + jnp.log2(o[HD : HD + 1])) for o, m in zip(outs, tops)]


def attend_back(jobs):
    weights = [jnp.exp2(tdot(kf, qf)) for kf, _, _, qf, _, _ in jobs]
    slopes = [tdot(v3, gf) for _, _, v3, _, _, gf in jobs]
    ds = [(p * dp).astype(bf16) for p, dp in zip(weights, slopes)]
    ps = [p.astype(bf16) for p in weights]
    return [(ndot(k, d), bdot(q, d), bdot(gf[:HD], p)) for (_, k, _, _, q, gf), d, p in zip(jobs, ds, ps)]


def gradient_side(grad, dd):
    row = lax.broadcasted_iota(jnp.int32, (16, grad.shape[1]), 0)
    f = jnp.zeros((16, grad.shape[1]), f32)
    for r, part in enumerate(split3(dd)):
        f = jnp.where(row == r, -part, f)
    return jnp.concatenate([grad, f.astype(bf16)], axis=0)


TILE = 256
TILES = [slice(at, at + TILE) for at in range(0, T, TILE)]


def head_of(ref, i, rows=HD):
    return ref[i * rows : (i + 1) * rows]


def near_kernel(q_ref, k_ref, v_ref, docs_ref, o_ref, lm_ref):
    docs = docs_ref[...]
    jobs = []
    for i in range(NEAR):
        g = pl.program_id(0) * NEAR + i
        kf = key_side(g, head_of(k_ref, i), docs)
        v1 = ones_below(head_of(v_ref, i), 1)
        q = head_of(q_ref, i)
        jobs += [(kf, v1, query_side(g, q[:, c], docs[:, c], positions(c.start, TILE, T), 0)) for c in TILES]
    done = attend(jobs)
    for i in range(NEAR):
        for c in TILES:
            o, lm = done.pop(0)
            o_ref[i * HD : (i + 1) * HD, c] = o
            lm_ref[i, :, c] = lm


def window(ref, g, level):
    w = T >> min(level, 2)
    at = pl.multiple_of((g >> (4 - min(level, 2))) * w, 128)
    return jnp.concatenate([ref[:, pl.ds(at, w)], ref[:, pl.ds(T + at, w)]], axis=1)


def guest_side(g, level, q, docs_ref, lm=None):
    width = T >> level
    block = g >> (4 - level)
    rows = docs_ref[...].astype(f32)
    pick = lax.broadcasted_iota(jnp.int32, rows.shape, 0) == block
    docs = jnp.sum(jnp.where(pick, rows, 0.0), axis=0, keepdims=True).astype(jnp.int32)
    return query_side(g, q, docs, positions(block * width, q.shape[1], width), level, lm)


def parcel(features, numbers, rows):
    parts = [p for row in numbers for p in split3(row)]
    rest = rows - FAR * HD - len(parts)
    stats = jnp.concatenate(parts + [jnp.zeros((rest, numbers[0].shape[1]), f32)], axis=0).astype(bf16)
    return jnp.concatenate(features + [stats], axis=0)


def number(block, i):
    rows = block[FAR * HD + 3 * i : FAR * HD + 3 * i + 3].astype(f32)
    return rows[0:1] + rows[1:2] + rows[2:3]


def far_kernel(levels, k_ref, v_ref, docs_ref, *refs):
    kf_ref = refs[-1]
    ins, outs = refs[: 2 * len(levels)], refs[2 * len(levels) : -1]
    jobs = []
    for i in range(FAR):
        g = pl.program_id(0) * FAR + i
        kf_ref[i] = key_side(g, head_of(k_ref, i), docs_ref[...])
        rows = pl.ds(i * HD, HD)
        for j, level in enumerate(levels):
            qf = guest_side(g, level, head_of(ins[2 * j], i), ins[2 * j + 1])
            jobs.append((window(kf_ref.at[i], g, level), ones_below(window(v_ref.at[rows], g, level), 1), qf))
    done = attend(jobs)
    for j, out in enumerate(outs):
        mine = done[j :: len(outs)]
        out[...] = parcel([o.astype(bf16) for o, _ in mine], [lm for _, lm in mine], BACK)


def near_back_kernel(first, q_ref, k_ref, v_ref, docs_ref, g_ref, lm_ref, dd_ref, *refs):
    gq_ref, gk_ref, gv_ref = refs[-3:]
    docs = docs_ref[...]
    jobs = []
    for i in range(NEAR):
        g = pl.program_id(0) * NEAR + i + first
        k, q, grad, lm, dd = head_of(k_ref, i), head_of(q_ref, i), head_of(g_ref, i), lm_ref[i], dd_ref[i]
        kf = key_side(g, k, docs)
        v3 = ones_below(head_of(v_ref, i), 3)
        for c in TILES:
            qf = query_side(g, q[:, c], docs[:, c], positions(c.start, TILE, T), 0, lm[:, c])
            jobs.append((kf, k, v3, qf, q[:, c], gradient_side(grad[:, c], dd[:, c])))
    done = attend_back(jobs)
    for i in range(NEAR):
        rows = slice(i * HD, (i + 1) * HD)
        mine = [done.pop(0) for _ in TILES]
        for c, (dq, _, _) in zip(TILES, mine):
            gq_ref[rows, c] = (dq * SCALE).astype(bf16)
        gk_ref[rows] = (sum(d[1] for d in mine) * SCALE).astype(bf16)
        gv_ref[rows] = sum(d[2] for d in mine).astype(bf16)


def far_back_kernel(levels, k_ref, v_ref, docs_ref, *refs):
    kf_ref, ak_ref, av_ref = refs[-3:]
    n = len(levels)
    ins, outs = refs[: 3 * n], refs[3 * n : -3]
    parcels = [ref[...] for ref in ins[2::3]]
    jobs = []
    for i in range(FAR):
        g = pl.program_id(0) * FAR + i
        kf_ref[i] = key_side(g, head_of(k_ref, i), docs_ref[...])
        rows = pl.ds(i * HD, HD)
        for j, level in enumerate(levels):
            q_ref, dq_ref = ins[3 * j : 3 * j + 2]
            q, grad = head_of(q_ref, i), head_of(parcels[j], i)
            qf = guest_side(g, level, q, dq_ref, number(parcels[j], 2 * i))
            gf = gradient_side(grad, number(parcels[j], 2 * i + 1))
            k, v = window(k_ref.at[rows], g, level), window(v_ref.at[rows], g, level)
            jobs.append((window(kf_ref.at[i], g, level), k, ones_below(v, 3), qf, q, gf))
    done = attend_back(jobs)
    ak_ref[...] = jnp.zeros_like(ak_ref)
    av_ref[...] = jnp.zeros_like(av_ref)
    for i in range(FAR):
        g = pl.program_id(0) * FAR + i
        rows = slice(i * HD, (i + 1) * HD)
        for j, level in enumerate(levels):
            dq, dk, dv = done.pop(0)
            outs[2 + j][rows] = (dq * SCALE).astype(bf16)
            w = T >> min(level, 2)
            at = (g >> (4 - min(level, 2))) * w
            for c in range(2):
                cols = pl.ds(pl.multiple_of(c * T + at, 128), w)
                ak_ref[rows, cols] += dk[:, c * w : (c + 1) * w]
                av_ref[rows, cols] += dv[:, c * w : (c + 1) * w]
    outs[0][...] = (ak_ref[...] * SCALE).astype(bf16)
    outs[1][...] = av_ref[...].astype(bf16)


NEAR, FAR = 4, 4
BACK, OUT = FAR * HD + 16, FAR * HD + 32


def head_rows(n, heads, first=0, rows=HD):
    return pl.BlockSpec((rows * heads, n), lambda i: (i + first // heads, 0))


def head_stats(n, heads, first=0):
    return pl.BlockSpec((heads, 1, n), lambda i: (i + first // heads, 0, 0))


def whole(*shape):
    return pl.BlockSpec(shape, lambda i: (0,) * len(shape))


def guest_docs(n):
    return pl.BlockSpec((16, n), lambda i: (D // 16, 0))


def shape_of(*dims, dtype=bf16):
    return jax.ShapeDtypeStruct(dims, dtype)


def attend_near(q, k, v, docs):
    r = lambda n: head_rows(n, NEAR)
    return kernel_call(
        near_kernel,
        grid=(HEADS // NEAR,),
        in_specs=[r(T), r(2 * T), r(2 * T), whole(1, 2 * T)],
        out_specs=[r(T), head_stats(T, NEAR)],
        out_shape=[shape_of(D, T, dtype=f32), shape_of(HEADS, 1, T, dtype=f32)],
        cost_estimate=cost(1),
        name="near",
    )(q, k, v, docs)


def attend_far(k, v, docs, guests, after):
    r = lambda n: head_rows(n, FAR)
    in_specs = [r(2 * T), r(2 * T), whole(1, 2 * T)]
    out_specs, out_shape, args = [], [], []
    for level, q in guests:
        n = q.shape[1]
        in_specs += [r(n), guest_docs(n)]
        out_specs.append(head_rows(n, 1, 0, BACK))
        out_shape.append(shape_of(BACK * HEADS // FAR, n))
        args += [q, q]
    return kernel_call(
        functools.partial(far_kernel, [v[0] for v in guests]),
        after=after,
        grid=(HEADS // FAR,),
        in_specs=in_specs,
        out_specs=out_specs,
        out_shape=out_shape,
        scratch_shapes=[pltpu.VMEM((FAR, 128, 2 * T), bf16)],
        cost_estimate=cost(1),
        name="far",
    )(k, v, docs, *args)


def near_back(q, k, v, docs, grads, lm, dd, first, count, rest=(), after=()):
    r = lambda n: head_rows(n, NEAR, first)
    return kernel_call(
        functools.partial(near_back_kernel, first),
        after=after,
        grid=(count // NEAR,),
        in_specs=[r(T), r(2 * T), r(2 * T), whole(1, 2 * T), r(T), head_stats(T, NEAR, first), head_stats(T, NEAR, first)] + [HB] * len(rest),
        out_specs=[r(T), r(2 * T), r(2 * T)],
        out_shape=[shape_of(D, n) for n in (T, 2 * T, 2 * T)],
        input_output_aliases={len(after) + 7 + i: i for i in range(len(rest))},
        cost_estimate=cost(1),
        name="near_back",
    )(q, k, v, docs, grads, lm, dd, *rest)


def far_back(k, v, docs, guests, after):
    r = lambda n: head_rows(n, FAR)
    in_specs = [r(2 * T), r(2 * T), whole(1, 2 * T)]
    out_specs, out_shape, args = [r(2 * T)] * 2, [shape_of(D, 2 * T)] * 2, []
    for level, q, grads in guests:
        n = q.shape[1]
        in_specs += [r(n), guest_docs(n), head_rows(n, 1, 0, OUT)]
        out_specs.append(r(n))
        out_shape.append(shape_of(D, n))
        args += [q, q, grads]
    return kernel_call(
        functools.partial(far_back_kernel, [v[0] for v in guests]),
        after=after,
        grid=(HEADS // FAR,),
        in_specs=in_specs,
        out_specs=out_specs,
        out_shape=out_shape,
        scratch_shapes=[pltpu.VMEM((FAR, 128, 2 * T), bf16), pltpu.VMEM((FAR * HD, 2 * T), f32), pltpu.VMEM((FAR * HD, 2 * T), f32)],
        cost_estimate=cost(1),
        name="far_back",
    )(k, v, docs, *args)


def permutation():
    p = lax.broadcasted_iota(jnp.int32, (T, T), 0)
    o = lax.broadcasted_iota(jnp.int32, (T, T), 1)
    return jnp.where(o == p % 32 * RES + bit_reversed(p // 32), 1.0, 0.0).astype(bf16)


def normalized(x):
    center = jnp.mean(x, axis=-1, keepdims=True)
    centered = x - center
    rstd = lax.rsqrt(jnp.mean(centered * centered, axis=-1, keepdims=True) + EPS)
    return centered * rstd, rstd


def norm_pullback(grad, xhat, rstd, gain):
    g = grad * gain
    gx = rstd * (g - jnp.mean(g, axis=-1, keepdims=True) - xhat * jnp.mean(g * xhat, axis=-1, keepdims=True))
    return gx, jnp.sum(grad * xhat, axis=0, keepdims=True), jnp.sum(grad, axis=0, keepdims=True)


def fetch(shards, buffer, sems, where_ref, rows):
    out = []
    for r, shard in enumerate(shards):
        at = pl.multiple_of(where_ref[r] * rows, rows)
        out.append(pltpu.make_async_copy(shard.at[pl.ds(0, rows)], buffer.at[pl.ds(at, rows)], sems.at[r]))
        out[-1].start()
    return out


def add_bias(values, row_ref, r):
    pick = jnp.where(lax.broadcasted_iota(jnp.int32, (16, values.shape[1]), 0) == r, 1.0, 0.0).astype(bf16)
    return values + tdot(row_ref, pick)


def block_lanes(g, level):
    at = g // (RES >> level) * (T >> level)
    return slice(at, at + (T >> level))


def head_slice(g):
    return slice(g * HD, (g + 1) * HD)


def project_kernel(levels, where_ref, w0, w1, w2, w3, vec_ref, bias_ref, docs_ref, x0_ref, x1_ref, *refs):
    q_ref, k_ref, v_ref, n_ref, in_ref, dout_ref = refs[:6]
    visit_refs = refs[6 : 5 + levels]
    w_ref, wt_ref, sems = refs[5 + levels :]
    copies = fetch((w0, w1, w2, w3), w_ref, sems, where_ref, D // 4)
    perm = permutation()
    gain, shift = vec_ref[0:1], vec_ref[2:3]

    def norm(x):
        xhat, _ = normalized(x.astype(f32))
        return ndot(perm, (xhat * gain + shift).astype(bf16)).astype(bf16)

    in_ref[...] = ndot(perm, x0_ref[...]).astype(bf16)
    n_ref[:T] = norm(x0_ref[...])
    n_ref[T:] = norm(x1_ref[:T])
    own_docs = bdot(jnp.broadcast_to(docs_ref[...].astype(f32), (8, T)).astype(bf16), perm)[0:1]
    near_docs = bdot(x1_ref[T:, :T], perm)[0:1]
    dout_ref[...] = jnp.concatenate([own_docs, near_docs], axis=1).astype(jnp.int32)
    for c in copies:
        c.wait()
    for part in range(3):
        wt = w_ref[:, part * D : (part + 1) * D].T
        for g in range(HEADS):
            h = int(ORDER[g])
            wt_ref[part * D + g * HD : part * D + (g + 1) * HD, :] = wt[head_slice(h)]
    n = n_ref[...]
    q_ref[...] = add_bias(bdot(wt_ref[:D, :], n_ref[:T]), bias_ref[...], 0).astype(bf16)
    for level in range(1, levels):
        width = T >> level
        visit = visit_refs[level - 1]
        for g in range(HEADS):
            visit[head_slice(g), :] = q_ref[head_slice(g), block_lanes(g, level)]
        rows = [own_docs[:, b * width : (b + 1) * width] for b in range(1 << level)]
        if level < 4:
            rows.append(jnp.zeros((16 - len(rows), width), f32))
        visit[D:, :] = jnp.concatenate(rows, axis=0).astype(bf16)
    k_ref[...] = bdot(wt_ref[D : 2 * D, :], n).astype(bf16)
    v_ref[...] = add_bias(bdot(wt_ref[2 * D :, :], n), bias_ref[...], 1).astype(bf16)


def project(levels, where, shards, vectors, biases, docs, tile, tile_near):
    return kernel_call(
        functools.partial(project_kernel, levels),
        in_specs=[SM] + [HB] * 4 + [VM] * 5,
        out_specs=[VM] * (5 + levels),
        out_shape=[shape_of(D, T), shape_of(D, 2 * T), shape_of(D, 2 * T), shape_of(2 * T, D), shape_of(T, D), shape_of(1, 2 * T, dtype=jnp.int32)]
        + [shape_of(D + 16, T >> level) for level in range(1, levels)],
        scratch_shapes=[pltpu.VMEM((D, 3 * D), bf16), pltpu.VMEM((3 * D, D), bf16), pltpu.SemaphoreType.DMA((4,))],
        cost_estimate=cost(1),
        name="project",
    )(where, *shards, vectors, biases, docs, tile, tile_near)


ERF_TOP = (0.00022905065861350646, 0.0034082910107109506, 0.050955695062380861, 0.18520832239976145, 1.128379143519084)
ERF_BOTTOM = (-1.1791602954361697e-7, 0.000023547966471313185, 0.0010179625278914885, 0.014070470171167667, 0.11098505178285362, 0.49746925110067538, 1.0)


def erf(x):
    x = jnp.clip(x, -3.7439211627767994, 3.7439211627767994)
    y = x * x
    top, bottom = ERF_TOP[0], ERF_BOTTOM[0]
    for c in ERF_TOP[1:]:
        top = top * y + c
    for c in ERF_BOTTOM[1:]:
        bottom = bottom * y + c
    return x * top / bottom


FF_PART = 768
FF_ROWS = 2 * FF_PART + D // 4


def merge_heads(o_ref, lm_ref, back, merged_ref, lmf_ref):
    for g in range(HEADS):
        base = lm_ref[g]
        parts, top = [], base
        blocks = [head_of(ref, g // FAR, BACK) for _, ref in back]
        for (level, _), block in zip(back, blocks):
            cols = block_lanes(g, level)
            rest = [jnp.full((1, n), -BIG, f32) for n in (cols.start, T - cols.stop)]
            parts.append(jnp.concatenate([x for x in (rest[0], number(block, g % FAR), rest[1]) if x.shape[1]], axis=1))
            top = jnp.maximum(top, parts[-1])
        weights = [jnp.exp2(x - top) for x in [base] + parts]
        total = sum(weights)
        scale = 1.0 / total
        out = o_ref[head_slice(g), :] * (weights[0] * scale)
        for (level, _), block, w in zip(back, blocks, weights[1:]):
            cols = block_lanes(g, level)
            add = head_of(block, g % FAR).astype(f32) * (w * scale)[:, cols]
            rest = [jnp.zeros((HD, n), f32) for n in (cols.start, T - cols.stop)]
            out = out + jnp.concatenate([x for x in (rest[0], add, rest[1]) if x.shape[1]], axis=1)
        merged_ref[head_slice(int(ORDER[g])), :] = out
        lmf_ref[g] = top + jnp.log2(total)


def middle_kernel(levels, back_levels, where_ref, *refs):
    shards, refs = refs[:4], refs[4:]
    o_ref, lm_ref, in_ref, cot_ref, vec_ref, hb_ref = refs[:6]
    n = len(back_levels)
    back = list(zip(back_levels, refs[6 : 6 + n]))
    refs = refs[6 + n :]
    enc_ref, mine_out, theirs_out, gm_ref, dd_ref, lmf_ref, gmid_ref, small_ref, gbias_ref = refs[:9]
    grad_out = lambda r, at, rows: (mine_out, theirs_out)[r % 2].at[r // 2, pl.ds(at, rows)]
    visit_refs, refs = refs[9 : 8 + levels], refs[8 + levels :]
    wo_ref, wu_ref, wd_ref, gd_ref, gu_ref, act_ref, merged_ref, y_ref, gn_ref, gy_ref, n2_ref, sems, osems = refs
    out_copies = fetch(shards, wo_ref, sems.at[0], where_ref, D // 4)
    up_copies, down_copies = [], []
    for r, shard in enumerate(shards):
        rows = pl.ds(pl.multiple_of(where_ref[r] * (D // 4), D // 4), D // 4)
        for c in range(4):
            dst = wu_ref.at[rows, pl.ds(c * FF_PART, FF_PART)]
            up_copies.append(pltpu.make_async_copy(shard.at[pl.ds((1 + c) * (D // 4), D // 4)], dst, sems.at[1 + c, r]))
            up_copies[-1].start()
    for r, shard in enumerate(shards):
        down_copies.append(pltpu.make_async_copy(shard.at[pl.ds(5 * (D // 4), FF_PART)], wd_ref.at[r], sems.at[5, r]))
        down_copies[-1].start()
    perm = permutation()
    gy_ref[...] = ndot(perm, cot_ref[...]).astype(bf16)
    merge_heads(o_ref, lm_ref, back, merged_ref, lmf_ref)
    merged = merged_ref[...].astype(bf16)
    for c in out_copies:
        c.wait()
    middle = in_ref[...].astype(f32) + tdot(merged, wo_ref[...]) + vec_ref[5:6]
    xhat, rstd = normalized(middle)
    n2_ref[...] = (xhat * vec_ref[1:2] + vec_ref[6:7]).astype(bf16)
    y_ref[...] = middle + vec_ref[7:8]
    gn_ref[...] = jnp.zeros_like(gn_ref)
    for c in up_copies:
        c.wait()
    down_parts = []
    for r in range(4):
        at = pl.multiple_of(where_ref[r] * FF_PART, FF_PART)
        cols = pl.ds(at, FF_PART)
        down_copies[r].wait()
        n2, gy = n2_ref[...], gy_ref[...]
        hidden = ndot(n2, wu_ref[:, cols]) + hb_ref[:, cols]
        phi = 0.5 + 0.5 * erf(hidden * 0.5**0.5)
        slope = phi + hidden * (jnp.exp(hidden * hidden * -0.5) * (2 * math.pi) ** -0.5)
        active = (hidden * phi).astype(bf16)
        y_ref[...] += ndot(active, wd_ref[r])
        gd_ref[r] = tdot(active, gy).astype(bf16)
        down_parts.append(pltpu.make_async_copy(gd_ref.at[r], grad_out(r, 0, FF_PART), osems.at[r]))
        down_parts[-1].start()
        gh = (slope * bdot(gy, wd_ref[r])).astype(bf16)
        gbias_ref[:, cols] = jnp.sum(gh.astype(f32), axis=0, keepdims=True)
        gu_ref[:, cols] = tdot(n2, gh).astype(bf16)
        gn_ref[...] += bdot(gh, wu_ref[:, cols])
    up_parts = []
    for r in range(4):
        at = pl.multiple_of(where_ref[r] * (D // 4), D // 4)
        for c in range(4):
            src = gu_ref.at[pl.ds(at, D // 4), pl.ds(c * FF_PART, FF_PART)]
            up_parts.append(pltpu.make_async_copy(src, grad_out(r, FF_PART + (1 + c) * (D // 4), D // 4), osems.at[8 + 4 * r + c]))
            up_parts[-1].start()
    enc_ref[...] = tdot(perm, y_ref[...].astype(bf16)).astype(bf16)
    gy = gy_ref[...].astype(f32)
    middle = in_ref[...].astype(f32) + tdot(merged, wo_ref[...]) + vec_ref[5:6]
    xhat, rstd = normalized(middle)
    gx, ggain, gshift = norm_pullback(gn_ref[...], xhat, rstd, vec_ref[1:2])
    gmid = gy + gx
    gmid_ref[...] = gmid
    gatt = gmid.astype(bf16)
    act_ref[...] = ndot(merged, gatt).astype(bf16)
    for r in range(4):
        at = pl.multiple_of(where_ref[r] * (D // 4), D // 4)
        down_parts.append(pltpu.make_async_copy(act_ref.at[pl.ds(at, D // 4)], grad_out(r, FF_PART, D // 4), osems.at[4 + r]))
        down_parts[-1].start()
    gm = bdot(wo_ref[...], gatt)
    prod = gm * merged_ref[...]
    gm = gm.astype(bf16)
    dds = [None] * HEADS
    for g in range(HEADS):
        h = head_slice(int(ORDER[g]))
        gm_ref[head_slice(g), :] = gm[h]
        dds[g] = jnp.sum(prod[h], axis=0, keepdims=True)
        dd_ref[g] = dds[g]
    for level in range(1, levels):
        for first in range(0, HEADS, FAR):
            features, numbers = [], []
            for g in range(first, first + FAR):
                cols = block_lanes(g, level)
                features.append(gm[head_slice(int(ORDER[g])), cols])
                numbers += [lmf_ref[g][:, cols], dds[g][:, cols]]
            at = first // FAR * OUT
            visit_refs[level - 1][at : at + OUT, :] = parcel(features, numbers, OUT)
    zero = jnp.zeros((4, D), f32)
    small_ref[...] = jnp.concatenate(
        [ggain, jnp.sum(gatt.astype(f32), axis=0, keepdims=True), gshift, jnp.sum(gy, axis=0, keepdims=True), zero], axis=0)
    for c in down_parts + up_parts:
        c.wait()


def middle(levels, where, shards, o, lm, back, inputs, cotangent, vectors, bias, after):
    s = shape_of
    ff = bias.shape[1]
    visits = [s(OUT * HEADS // FAR, T >> level) for level in range(1, levels)]
    return kernel_call(
        functools.partial(middle_kernel, levels, [b[0] for b in back]),
        after=after,
        in_specs=[SM] + [HB] * 4 + [VM] * (6 + len(back)),
        out_specs=[VM] + [HB] * 2 + [VM] * (6 + len(visits)),
        out_shape=[
            s(T, D), s(2, FF_ROWS, D), s(2, FF_ROWS, D),
            s(D, T), s(HEADS, 1, T, dtype=f32), s(HEADS, 1, T, dtype=f32), s(T, D, dtype=f32), s(8, D, dtype=f32), s(1, ff, dtype=f32),
        ] + visits,
        scratch_shapes=[
            pltpu.VMEM((D, D), bf16), pltpu.VMEM((D, ff), bf16), pltpu.VMEM((4, FF_PART, D), bf16),
            pltpu.VMEM((4, FF_PART, D), bf16), pltpu.VMEM((D, ff), bf16), pltpu.VMEM((D, D), bf16), pltpu.VMEM((D, T), f32),
            pltpu.VMEM((T, D), f32), pltpu.VMEM((T, D), f32), pltpu.VMEM((T, D), bf16), pltpu.VMEM((T, D), bf16),
            pltpu.SemaphoreType.DMA((6, 4)), pltpu.SemaphoreType.DMA((24,)),
        ],
        cost_estimate=cost(1),
        name="middle",
    )(where, *shards, o, lm, inputs, cotangent, vectors, bias, *[b[1] for b in back])


def natural(refs):
    rows = []
    for h in range(HEADS):
        g = head_slice(int(ORDER[h]))
        rows.append(sum(ref[g, :].astype(f32) for ref in refs).astype(bf16))
    return jnp.concatenate(rows, axis=0)


def to_blocks(where_ref, src_ref, out_refs, parts):
    rows = D // 4
    for r in range(4):
        at = pl.multiple_of(where_ref[r] * rows, rows)
        for part in range(parts):
            out_refs[r % 2][r // 2, part * rows : (part + 1) * rows, :] = src_ref[pl.ds(at, rows), part * D : (part + 1) * D]


def keys_kernel(where_ref, w0, w1, w2, w3, nk_ref, nv_ref, fk_ref, fv_ref, n_ref, vec_ref,
                send_ref, own_ref, mine_ref, theirs_ref, sums_ref, w_ref, gp_ref, gw_ref, sems):
    copies = fetch((w0, w1, w2, w3), w_ref, sems, where_ref, D // 4)
    gp_ref[:D] = natural((nk_ref, fk_ref))
    gp_ref[D:] = natural((nv_ref, fv_ref))
    for c in copies:
        c.wait()
    send = xdot(gp_ref[:, T:], w_ref[:, D:])
    send_ref[...] = send.astype(bf16)
    gw_ref[...] = xdot(n_ref[...], gp_ref[...]).astype(bf16)
    to_blocks(where_ref, gw_ref, (mine_ref, theirs_ref), 2)
    own_ref[...] = xdot(gp_ref[:, :T], w_ref[:, D:])
    xhat = (n_ref[T:].astype(f32) - vec_ref[2:3]) / vec_ref[0:1]
    rows = [bdot(jnp.ones((16, 2 * T), bf16), gp_ref[D:, :])[0:1]]
    rows += [jnp.sum(send * xhat, axis=0, keepdims=True), jnp.sum(send, axis=0, keepdims=True), jnp.zeros((5, D), f32)]
    sums_ref[...] = jnp.concatenate(rows, axis=0)


def keys_last(where, shards, grads, normed, vectors, after):
    s = shape_of
    return kernel_call(
        keys_kernel,
        after=after,
        in_specs=[SM] + [HB] * 4 + [VM] * 6,
        out_specs=[VM] * 5,
        out_shape=[s(T, D), s(T, D, dtype=f32), s(2, D // 2, D), s(2, D // 2, D), s(8, D, dtype=f32)],
        scratch_shapes=[pltpu.VMEM((D, 3 * D), bf16), pltpu.VMEM((2 * D, 2 * T), bf16), pltpu.VMEM((D, 2 * D), bf16), pltpu.SemaphoreType.DMA((4,))],
        cost_estimate=cost(1),
        name="keys_last",
    )(where, *shards, *grads, normed, vectors)


LAST_ROWS = 256


def queries_kernel(back_levels, where_ref, w0, w1, w2, w3, gq_ref, *refs):
    back = list(zip(back_levels, refs))
    n_ref, in_ref, vec_ref, small_ref, gbias_ref, own_ref, sums_ref = refs[len(back) : len(back) + 7]
    grad_ref, mine_ref, theirs_ref, w_ref, gp_ref, gw_ref, sems = refs[len(back) + 7 :]
    copies = fetch((w0, w1, w2, w3), w_ref, sems, where_ref, D // 4)
    for g in range(HEADS):
        rows = head_slice(g)
        total = gq_ref[rows, :].astype(f32)
        for level, ref in back:
            cols = block_lanes(g, level)
            rest = [jnp.zeros((HD, n), f32) for n in (cols.start, T - cols.stop)]
            total = total + jnp.concatenate([x for x in (rest[0], ref[rows, :].astype(f32), rest[1]) if x.shape[1]], axis=1)
        gp_ref[head_slice(int(ORDER[g])), :] = total.astype(bf16)
    gw_ref[...] = xdot(n_ref[:T], gp_ref[...]).astype(bf16)
    to_blocks(where_ref, gw_ref, (mine_ref, theirs_ref), 1)
    sums = bdot(jnp.ones((16, T), bf16), gp_ref[...])
    xhat, _ = normalized(in_ref[...].astype(f32))
    for c in copies:
        c.wait()
    grad = xdot(gp_ref[...], w_ref[:, :D]) + own_ref[...]
    grad_ref[...] = grad
    ggain = jnp.sum(grad * xhat, axis=0, keepdims=True) + sums_ref[1:2]
    gshift = jnp.sum(grad, axis=0, keepdims=True) + sums_ref[2:3]
    rows = [ggain, small_ref[0:1], gshift, sums[0:1], sums_ref[0:1], small_ref[1:4]]
    rows += [gbias_ref[:, i * D : (i + 1) * D] for i in range(4)]
    rows += [jnp.zeros((4, D), f32)]
    small = jnp.concatenate(rows, axis=0).astype(bf16)
    for out in (mine_ref, theirs_ref):
        for r in range(2):
            out[r, D // 4 : D // 4 + 16, :] = small
            out[r, D // 4 + 16 :, :] = jnp.zeros((LAST_ROWS - D // 4 - 16, D), bf16)


def queries_last(where, shards, gq, back, normed, inputs, vectors, small, gbias, own, sums, after):
    return kernel_call(
        functools.partial(queries_kernel, [b[0] for b in back]),
        after=after,
        in_specs=[SM] + [HB] * 4 + [VM] * (8 + len(back)),
        out_specs=[VM] * 3,
        out_shape=[shape_of(T, D, dtype=f32), shape_of(2, LAST_ROWS, D), shape_of(2, LAST_ROWS, D)],
        scratch_shapes=[pltpu.VMEM((D, 3 * D), bf16), pltpu.VMEM((D, T), bf16), pltpu.VMEM((D, D), bf16), pltpu.SemaphoreType.DMA((4,))],
        cost_estimate=cost(1),
        name="queries_last",
    )(where, *shards, gq, *[b[1] for b in back], normed, inputs, vectors, small, gbias, own, sums)


def last_kernel(grad_ref, in_ref, gmid_ref, vec_ref, got_ref, gt_ref):
    xhat, rstd = normalized(in_ref[...].astype(f32))
    gx, _, _ = norm_pullback(grad_ref[...] + got_ref[...].astype(f32), xhat, rstd, vec_ref[0:1])
    gt_ref[...] = tdot(permutation(), (gmid_ref[...] + gx).astype(bf16)).astype(bf16)


def last(grad, inputs, gmid, vectors, got, after):
    return kernel_call(
        last_kernel,
        after=after,
        in_specs=[VM] * 5,
        out_specs=VM,
        out_shape=shape_of(T, D),
        cost_estimate=cost(1),
        name="last",
    )(grad, inputs, gmid, vectors, got)


def gate_kernel(*refs):
    refs[-1][...] = jnp.zeros_like(refs[-1])


def gate(arrays, us):
    return kernel_call(
        gate_kernel,
        in_specs=[HB] * len(arrays),
        out_specs=VM,
        out_shape=shape_of(8, 128, dtype=f32),
        cost_estimate=cost(us),
        name="gate",
    )(*arrays)


def exchanged(x, axis, mask):
    return lax.ppermute(x, axis, [(i, i ^ mask) for i in range(lax.axis_size(axis))])


def added(a, b):
    return (a.astype(f32) + b.astype(f32)).astype(bf16)


def behind(x, other):
    return lax.optimization_barrier((x, other))[0]


class Chain:
    def __init__(self, line, steps):
        self.line, self.steps = line, list(steps)

    def begin(self, value, theirs=None):
        self.value = value
        self.launch(theirs)
        return self

    def launch(self, theirs=None):
        x, line = self.value, self.line
        if not self.steps:
            return
        step = self.steps[0]
        if step == "c":
            self.kept, self.got = x, exchanged(theirs, "fsdp", 1)
        elif step == "x":
            self.kept, self.got = x[:1], exchanged(x[1:], "fsdp", 2)
        elif step == "a":
            self.got = lax.all_to_all(x.reshape(line.seq, -1, D), "seq", 0, 0)
        elif step == "g":
            self.got = lax.all_to_all(jnp.broadcast_to(x, (line.seq,) + x.shape[1:]), "seq", 0, 0)
        elif step in ("F0", "F1", "F2"):
            self.kept, self.got = x, exchanged(x, "seq", 1 << int(step[1]))
        elif isinstance(step, int):
            half = x.shape[1] // 2
            mine = line.rank >> step & 1
            self.kept = lax.dynamic_slice_in_dim(x, mine * half, half, 1)
            self.got = exchanged(lax.dynamic_slice_in_dim(x, (1 - mine) * half, half, 1), "seq", 1 << step)
        else:
            self.got = exchanged(x, "seq", 1 << int(step))

    def advance(self):
        step, got = self.steps.pop(0), behind(self.got, self.line.token)
        if step == "a":
            out = jnp.sum(got.astype(f32), axis=0, keepdims=True).astype(bf16)
        elif step == "g":
            out = got.reshape(1, -1, D)
        elif isinstance(step, str) and step.isdigit():
            x, low = self.value, (self.line.rank >> int(step) & 1) == 0
            out = jnp.concatenate([jnp.where(low, x, got), jnp.where(low, got, x)], axis=1)
        else:
            out = added(self.kept, got)
            if step == "x":
                for bit in range(3, self.line.seq.bit_length() - 1):
                    if "a" not in self.steps:
                        out = added(out, exchanged(out, "seq", 1 << bit))
        self.value = self.line.token = out
        self.launch()


class Line:
    def __init__(self, rank, seq, token):
        self.rank, self.seq, self.token = rank, seq, token


def local(tiles, documents, cotangent, w_qkv, w_out, w_up, w_down, gains, shifts, hidden_bias):
    seq = lax.axis_size("seq")
    rank = lax.axis_index("seq")
    part = lax.axis_index("fsdp")
    levels = min(BRANCHES, (seq * T // SEG_BASE).bit_length())
    where = jnp.stack([part ^ r for r in range(4)]).astype(jnp.int32)
    visits = [(level, (1 << level) + 2 * c) for level in range(1, levels) for c in range(1 << level - 1)]
    cols = gains.shape[1]

    packed = jnp.concatenate([gains, shifts, hidden_bias.reshape(-1, cols)], axis=0).reshape(1, -1)
    w_ext = jnp.concatenate([w_qkv, jnp.pad(packed, ((0, 7), (0, 0)))], axis=0)
    qkv_far = exchanged(w_ext, "fsdp", 2)
    tile = tiles[0]
    docs_row = jnp.pad(documents.astype(bf16), ((0, 7), (0, D - T)))
    tile_near = exchanged(jnp.concatenate([tile, docs_row], axis=0), "seq", 1)
    stacked_up = w_up.reshape(cols, -1, D).swapaxes(0, 1).reshape(-1, D)
    w_ff = jnp.concatenate([w_out, stacked_up, w_down], axis=0)
    ff_far = exchanged(w_ff, "fsdp", 2)
    qkv_near = exchanged(w_ext, "fsdp", 1)
    qkv_shards = (w_ext, qkv_near, qkv_far, exchanged(behind(qkv_far, tile_near), "fsdp", 1))
    ff_near = exchanged(w_ff, "fsdp", 1)

    stacked = jnp.stack([w[cols].reshape(-1, cols) for w in qkv_shards])
    in_order = jnp.stack([lax.dynamic_index_in_dim(stacked, part ^ s, 0, keepdims=False) for s in range(4)])
    rows = in_order[:, :8].transpose(1, 0, 2).reshape(8, D)
    vectors = rows.astype(f32)
    bias_row = in_order[:, 8:].reshape(1, -1).astype(f32)
    by_head = rows[3:5].reshape(2, 2, 2, 2, 2, HD).transpose(0, 4, 3, 2, 1, 5).reshape(2, D)
    biases = jnp.concatenate([by_head, jnp.zeros((14, D), bf16)], axis=0)

    q, k, v, normed, inputs, docs, *queries = project(levels, where, qkv_shards, vectors, biases, documents, tile, tile_near)
    guests = [(level, exchanged(queries[level - 1], "seq", mask)) for level, mask in visits]
    o, lm = attend_near(q, k, v, docs)
    partial = attend_far(k, v, docs, guests, [lm])
    back = [(level, exchanged(x, "seq", mask)) for (level, mask), x in zip(visits, partial)]
    shards = (w_ff, ff_near, ff_far, exchanged(behind(ff_far, [x for _, x in back]), "fsdp", 1))

    encoded, early_mine, early_theirs, gmerged, dd, lmf, gmid, small, gbias, *send = middle(
        levels, where, shards, o, lm, back, inputs, cotangent[0], vectors, bias_row, [])
    early_theirs = exchanged(early_theirs, "fsdp", 1)
    guests = [guest + (exchanged(send[level - 1], "seq", mask),) for guest, (level, mask) in zip(guests, visits)]
    nears = near_back(q, k, v, docs, gmerged, lmf, dd, 0, 4)
    early = added(early_mine, behind(early_theirs, nears[0]))
    n = FF_PART + D // 4
    line = Line(rank, seq, early)
    up = Chain(line, ["x", 1, 0, 2, "2", "0", "1"]).begin(early[:, n:])
    down = Chain(line, [0, "x", 1, 2, "2", "1", "0"]).begin(early[:, :n])
    keys = Chain(line, ["c", "x", 0, 1, 2, "2", "1", "0"])
    late = Chain(line, ["c", "x", "a", "g"])
    gq, gk, gv = near_back(q, k, v, docs, gmerged, lmf, dd, 4, 12, nears, [early])
    far_k, far_v, *turned = far_back(k, v, docs, guests, [gq])
    back = [(level, exchanged(x, "seq", mask)) for (level, mask), x in zip(visits, turned)]

    returned = gate([x for _, x in back], 30)

    line.token = far_k
    up.advance()
    down.advance()
    to_near, own_part, keys_mine, keys_theirs, sums = keys_last(
        where, qkv_shards, (gk, gv, far_k, far_v), normed, vectors, [line.token])
    got = exchanged(to_near, "seq", 1)
    keys.begin(keys_mine, keys_theirs)
    grad, late_mine, late_theirs = queries_last(
        where, qkv_shards, gq, back, normed, inputs, vectors, small, gbias, own_part, sums, [returned])
    late.begin(late_mine, late_theirs)
    line.token = late_mine
    for chain in (keys, up, late, down, up, late, keys, down, up, None, keys, down, up, late, keys, down, up, keys, down, keys, up, keys, late, down, keys):
        if chain is None:
            grad_tiles = line.token = last(grad, inputs, gmid, vectors, got, [line.token])
        else:
            chain.advance()
    sum_up, sum_down, late_keys, late = [c.value[0].astype(f32) for c in (up, down, keys, late)]

    side_by_side = lambda a: a.reshape(-1, D // 4, D).swapaxes(0, 1).reshape(D // 4, -1)
    tiny = late[D // 4 : D // 4 + 16]
    mine = lax.dynamic_slice_in_dim(tiny[:8], part * cols, cols, 1)
    sum_bias = lax.dynamic_slice_in_dim(tiny[8:12], part, 1, 0).reshape(-1)
    return (
        encoded[None],
        grad_tiles[None],
        side_by_side(jnp.concatenate([late[: D // 4], late_keys], axis=0)), sum_down[FF_PART:], side_by_side(sum_up), sum_down[:FF_PART],
        mine[:2], mine[2:], sum_bias,
    )


def solution(mesh):
    tokens, rows, cols = P("fsdp", "seq", None), P("fsdp", None), P(None, "fsdp")
    return jax.shard_map(
        local,
        mesh=mesh,
        in_specs=(tokens, P("fsdp", "seq"), tokens, rows, rows, rows, rows, cols, cols, P("fsdp")),
        out_specs=(tokens, tokens, rows, rows, rows, rows, cols, cols, P("fsdp")),
        check_vma=False,
    )
```

```python
import functools
import math

import jax
import jax.numpy as jnp
import ml_dtypes
import numpy as np
from jax import lax
from jax.experimental import pallas as pl
from jax.experimental.pallas import tpu as pltpu
from jax.sharding import PartitionSpec as P

HEADS = 16
HD = 48
D = HEADS * HD
SEG_BASE = 1024
BRANCHES = 5
T = 512
RES = 16
EPS = 1e-05
BIG = 2.0**100
SCALE = HD**-0.5
VMEM = 56 << 20
ORDER = np.array([int(f"{c:04b}"[::-1], 2) for c in range(RES)])
bf16, f32 = jnp.bfloat16, jnp.float32

VM = pl.BlockSpec(memory_space=pltpu.VMEM)
SM = pl.BlockSpec(memory_space=pltpu.SMEM)
HB = pl.BlockSpec(memory_space=pl.ANY)


def tdot(a, b):
    return lax.dot_general(a, b, (((0,), (0,)), ((), ())), preferred_element_type=f32)


def ndot(a, b):
    return lax.dot_general(a, b, (((1,), (0,)), ((), ())), preferred_element_type=f32)


def bdot(a, b):
    return lax.dot_general(a, b, (((1,), (1,)), ((), ())), preferred_element_type=f32)


def xdot(a, b):
    return lax.dot_general(a, b, (((0,), (1,)), ((), ())), preferred_element_type=f32)


def cost(us):
    return pl.CostEstimate(flops=int(us * 1e9), bytes_accessed=1000, transcendentals=0)


def kernel_call(body, in_specs, after=(), **kwargs):
    count = len(after)
    call = pl.pallas_call(
        (lambda *refs: body(*refs[count:])) if count else body,
        in_specs=[HB] * count + in_specs,
        compiler_params=pltpu.CompilerParams(vmem_limit_bytes=VMEM),
        **kwargs,
    )
    return functools.partial(call, *after)


def bit_reversed(h):
    return (h % 2) * 8 + (h // 2 % 2) * 4 + (h // 4 % 2) * 2 + h // 8


def split2(x):
    hi = x.astype(bf16)
    return hi, (x - hi.astype(f32)).astype(bf16)


def split3(x):
    a = x.astype(bf16).astype(f32)
    b = (x - a).astype(bf16).astype(f32)
    return a, b, x - a - b


def log_ratio(level):
    out = []
    for t in range(1, BRANCHES):
        c = math.log2((t + 1 - level) / (t - level)) if t > level else 0.0
        hi = float(np.asarray(c).astype(ml_dtypes.bfloat16))
        out.append((hi, float(np.asarray(c - hi).astype(ml_dtypes.bfloat16))))
    return out


def valuation(g, pos):
    c = pos >> 5
    hits = [((c >> n) == (g >> n)).astype(jnp.int32) for n in (3, 2, 1, 0)]
    return hits[0] + hits[1] + hits[2] + hits[3]


def query_side(g, q, docs, pos, level, lm=None):
    n = q.shape[1]
    hi, lo = split2(q.astype(f32) * (SCALE * math.log2(math.e)))
    row = lax.broadcasted_iota(jnp.int32, (32, n), 0)
    v = valuation(g, pos)
    f = jnp.where((row < 4) & (row == docs), -BIG, 0.0)
    for i, parts in enumerate(log_ratio(level)):
        for j, part in enumerate(parts):
            if part:
                f = jnp.where((row == 4 + 2 * i + j) & (v > i), part, f)
    if level >= 3:
        f = jnp.where(row == 12, -BIG, f)
    if level >= 4:
        f = jnp.where(row == 13, -BIG, f)
    if lm is not None:
        for r, part in enumerate(split3(lm)):
            f = jnp.where(row == 14 + r, -part, f)
    return jnp.concatenate([hi, lo, f.astype(bf16)], axis=0)


def key_side(g, k, docs):
    n = k.shape[1]
    pos = lax.broadcasted_iota(jnp.int32, (1, n), 1) & (T - 1)
    row = lax.broadcasted_iota(jnp.int32, (32, n), 0)
    v = valuation(g, pos)
    f = jnp.where((row < 4) & (row != docs), 1.0, 0.0)
    f = jnp.where((row >= 4) & (row < 12) & (v >= ((row - 2) >> 1)), 1.0, f)
    f = jnp.where((row == 12) & (v < 3), 1.0, f)
    f = jnp.where((row == 13) & (v < 4), 1.0, f)
    f = jnp.where((row >= 14) & (row < 17), 1.0, f)
    return jnp.concatenate([k, k, f.astype(bf16)], axis=0)


def ones_below(v, count):
    row = lax.broadcasted_iota(jnp.int32, (16, v.shape[1]), 0)
    return jnp.concatenate([v, jnp.where(row < count, 1.0, 0.0).astype(bf16)], axis=0)


def positions(first, n, width):
    return first + (lax.broadcasted_iota(jnp.int32, (1, n), 1) & (width - 1))


def attend(jobs):
    scores = [tdot(kf, qf) for kf, _, qf in jobs]
    tops = [jnp.max(s, axis=0, keepdims=True) for s in scores]
    weights = [jnp.exp2(s - m).astype(bf16) for s, m in zip(scores, tops)]
    outs = [ndot(v1, p) for (_, v1, _), p in zip(jobs, weights)]
    return [(o[:HD] * (1.0 / o[HD : HD + 1]), m + jnp.log2(o[HD : HD + 1])) for o, m in zip(outs, tops)]


def attend_back(jobs):
    weights = [jnp.exp2(tdot(kf, qf)) for kf, _, _, qf, _, _ in jobs]
    slopes = [tdot(v3, gf) for _, _, v3, _, _, gf in jobs]
    ds = [(p * dp).astype(bf16) for p, dp in zip(weights, slopes)]
    ps = [p.astype(bf16) for p in weights]
    return [(ndot(k, d), bdot(q, d), bdot(gf[:HD], p)) for (_, k, _, _, q, gf), d, p in zip(jobs, ds, ps)]


def gradient_side(grad, dd):
    row = lax.broadcasted_iota(jnp.int32, (16, grad.shape[1]), 0)
    f = jnp.zeros((16, grad.shape[1]), f32)
    for r, part in enumerate(split3(dd)):
        f = jnp.where(row == r, -part, f)
    return jnp.concatenate([grad, f.astype(bf16)], axis=0)


TILE = 256
TILES = [slice(at, at + TILE) for at in range(0, T, TILE)]


def head_of(ref, i, rows=HD):
    return ref[i * rows : (i + 1) * rows]


def near_kernel(q_ref, k_ref, v_ref, docs_ref, o_ref, lm_ref):
    docs = docs_ref[...]
    jobs = []
    for i in range(NEAR):
        g = pl.program_id(0) * NEAR + i
        kf = key_side(g, head_of(k_ref, i), docs)
        v1 = ones_below(head_of(v_ref, i), 1)
        q = head_of(q_ref, i)
        jobs += [(kf, v1, query_side(g, q[:, c], docs[:, c], positions(c.start, TILE, T), 0)) for c in TILES]
    done = attend(jobs)
    for i in range(NEAR):
        for c in TILES:
            o, lm = done.pop(0)
            o_ref[i * HD : (i + 1) * HD, c] = o
            lm_ref[i, :, c] = lm


def window(ref, g, level):
    w = T >> min(level, 2)
    at = pl.multiple_of((g >> (4 - min(level, 2))) * w, 128)
    return jnp.concatenate([ref[:, pl.ds(at, w)], ref[:, pl.ds(T + at, w)]], axis=1)


def guest_side(g, level, q, docs_ref, lm=None):
    width = T >> level
    block = g >> (4 - level)
    rows = docs_ref[...].astype(f32)
    pick = lax.broadcasted_iota(jnp.int32, rows.shape, 0) == block
    docs = jnp.sum(jnp.where(pick, rows, 0.0), axis=0, keepdims=True).astype(jnp.int32)
    return query_side(g, q, docs, positions(block * width, q.shape[1], width), level, lm)


def parcel(features, numbers, rows):
    parts = [p for row in numbers for p in split3(row)]
    rest = rows - FAR * HD - len(parts)
    stats = jnp.concatenate(parts + [jnp.zeros((rest, numbers[0].shape[1]), f32)], axis=0).astype(bf16)
    return jnp.concatenate(features + [stats], axis=0)


def number(block, i):
    rows = block[FAR * HD + 3 * i : FAR * HD + 3 * i + 3].astype(f32)
    return rows[0:1] + rows[1:2] + rows[2:3]


def far_kernel(levels, k_ref, v_ref, docs_ref, *refs):
    kf_ref = refs[-1]
    ins, outs = refs[: 2 * len(levels)], refs[2 * len(levels) : -1]
    jobs = []
    for i in range(FAR):
        g = pl.program_id(0) * FAR + i
        kf_ref[i] = key_side(g, head_of(k_ref, i), docs_ref[...])
        rows = pl.ds(i * HD, HD)
        for j, level in enumerate(levels):
            qf = guest_side(g, level, head_of(ins[2 * j], i), ins[2 * j + 1])
            jobs.append((window(kf_ref.at[i], g, level), ones_below(window(v_ref.at[rows], g, level), 1), qf))
    done = attend(jobs)
    for j, out in enumerate(outs):
        mine = done[j :: len(outs)]
        out[...] = parcel([o.astype(bf16) for o, _ in mine], [lm for _, lm in mine], BACK)


def near_back_kernel(first, q_ref, k_ref, v_ref, docs_ref, g_ref, lm_ref, dd_ref, *refs):
    gq_ref, gk_ref, gv_ref = refs[-3:]
    docs = docs_ref[...]
    jobs = []
    for i in range(NEAR):
        g = pl.program_id(0) * NEAR + i + first
        k, q, grad, lm, dd = head_of(k_ref, i), head_of(q_ref, i), head_of(g_ref, i), lm_ref[i], dd_ref[i]
        kf = key_side(g, k, docs)
        v3 = ones_below(head_of(v_ref, i), 3)
        for c in TILES:
            qf = query_side(g, q[:, c], docs[:, c], positions(c.start, TILE, T), 0, lm[:, c])
            jobs.append((kf, k, v3, qf, q[:, c], gradient_side(grad[:, c], dd[:, c])))
    done = attend_back(jobs)
    for i in range(NEAR):
        rows = slice(i * HD, (i + 1) * HD)
        mine = [done.pop(0) for _ in TILES]
        for c, (dq, _, _) in zip(TILES, mine):
            gq_ref[rows, c] = (dq * SCALE).astype(bf16)
        gk_ref[rows] = (sum(d[1] for d in mine) * SCALE).astype(bf16)
        gv_ref[rows] = sum(d[2] for d in mine).astype(bf16)


def far_back_kernel(levels, k_ref, v_ref, docs_ref, *refs):
    kf_ref, ak_ref, av_ref = refs[-3:]
    n = len(levels)
    ins, outs = refs[: 3 * n], refs[3 * n : -3]
    parcels = [ref[...] for ref in ins[2::3]]
    jobs = []
    for i in range(FAR):
        g = pl.program_id(0) * FAR + i
        kf_ref[i] = key_side(g, head_of(k_ref, i), docs_ref[...])
        rows = pl.ds(i * HD, HD)
        for j, level in enumerate(levels):
            q_ref, dq_ref = ins[3 * j : 3 * j + 2]
            q, grad = head_of(q_ref, i), head_of(parcels[j], i)
            qf = guest_side(g, level, q, dq_ref, number(parcels[j], 2 * i))
            gf = gradient_side(grad, number(parcels[j], 2 * i + 1))
            k, v = window(k_ref.at[rows], g, level), window(v_ref.at[rows], g, level)
            jobs.append((window(kf_ref.at[i], g, level), k, ones_below(v, 3), qf, q, gf))
    done = attend_back(jobs)
    ak_ref[...] = jnp.zeros_like(ak_ref)
    av_ref[...] = jnp.zeros_like(av_ref)
    for i in range(FAR):
        g = pl.program_id(0) * FAR + i
        rows = slice(i * HD, (i + 1) * HD)
        for j, level in enumerate(levels):
            dq, dk, dv = done.pop(0)
            outs[2 + j][rows] = (dq * SCALE).astype(bf16)
            w = T >> min(level, 2)
            at = (g >> (4 - min(level, 2))) * w
            for c in range(2):
                cols = pl.ds(pl.multiple_of(c * T + at, 128), w)
                ak_ref[rows, cols] += dk[:, c * w : (c + 1) * w]
                av_ref[rows, cols] += dv[:, c * w : (c + 1) * w]
    outs[0][...] = (ak_ref[...] * SCALE).astype(bf16)
    outs[1][...] = av_ref[...].astype(bf16)


NEAR, FAR = 4, 4
BACK, OUT = FAR * HD + 16, FAR * HD + 32


def head_rows(n, heads, first=0, rows=HD):
    return pl.BlockSpec((rows * heads, n), lambda i: (i + first // heads, 0))


def head_stats(n, heads, first=0):
    return pl.BlockSpec((heads, 1, n), lambda i: (i + first // heads, 0, 0))


def whole(*shape):
    return pl.BlockSpec(shape, lambda i: (0,) * len(shape))


def guest_docs(n):
    return pl.BlockSpec((16, n), lambda i: (D // 16, 0))


def shape_of(*dims, dtype=bf16):
    return jax.ShapeDtypeStruct(dims, dtype)


def attend_near(q, k, v, docs):
    r = lambda n: head_rows(n, NEAR)
    return kernel_call(
        near_kernel,
        grid=(HEADS // NEAR,),
        in_specs=[r(T), r(2 * T), r(2 * T), whole(1, 2 * T)],
        out_specs=[r(T), head_stats(T, NEAR)],
        out_shape=[shape_of(D, T, dtype=f32), shape_of(HEADS, 1, T, dtype=f32)],
        cost_estimate=cost(1),
        name="near",
    )(q, k, v, docs)


def attend_far(k, v, docs, guests, after):
    r = lambda n: head_rows(n, FAR)
    in_specs = [r(2 * T), r(2 * T), whole(1, 2 * T)]
    out_specs, out_shape, args = [], [], []
    for level, q in guests:
        n = q.shape[1]
        in_specs += [r(n), guest_docs(n)]
        out_specs.append(head_rows(n, 1, 0, BACK))
        out_shape.append(shape_of(BACK * HEADS // FAR, n))
        args += [q, q]
    return kernel_call(
        functools.partial(far_kernel, [v[0] for v in guests]),
        after=after,
        grid=(HEADS // FAR,),
        in_specs=in_specs,
        out_specs=out_specs,
        out_shape=out_shape,
        scratch_shapes=[pltpu.VMEM((FAR, 128, 2 * T), bf16)],
        cost_estimate=cost(1),
        name="far",
    )(k, v, docs, *args)


def near_back(q, k, v, docs, grads, lm, dd, first, count, rest=(), after=()):
    r = lambda n: head_rows(n, NEAR, first)
    return kernel_call(
        functools.partial(near_back_kernel, first),
        after=after,
        grid=(count // NEAR,),
        in_specs=[r(T), r(2 * T), r(2 * T), whole(1, 2 * T), r(T), head_stats(T, NEAR, first), head_stats(T, NEAR, first)] + [HB] * len(rest),
        out_specs=[r(T), r(2 * T), r(2 * T)],
        out_shape=[shape_of(D, n) for n in (T, 2 * T, 2 * T)],
        input_output_aliases={len(after) + 7 + i: i for i in range(len(rest))},
        cost_estimate=cost(1),
        name="near_back",
    )(q, k, v, docs, grads, lm, dd, *rest)


def far_back(k, v, docs, guests, after):
    r = lambda n: head_rows(n, FAR)
    in_specs = [r(2 * T), r(2 * T), whole(1, 2 * T)]
    out_specs, out_shape, args = [r(2 * T)] * 2, [shape_of(D, 2 * T)] * 2, []
    for level, q, grads in guests:
        n = q.shape[1]
        in_specs += [r(n), guest_docs(n), head_rows(n, 1, 0, OUT)]
        out_specs.append(r(n))
        out_shape.append(shape_of(D, n))
        args += [q, q, grads]
    return kernel_call(
        functools.partial(far_back_kernel, [v[0] for v in guests]),
        after=after,
        grid=(HEADS // FAR,),
        in_specs=in_specs,
        out_specs=out_specs,
        out_shape=out_shape,
        scratch_shapes=[pltpu.VMEM((FAR, 128, 2 * T), bf16), pltpu.VMEM((FAR * HD, 2 * T), f32), pltpu.VMEM((FAR * HD, 2 * T), f32)],
        cost_estimate=cost(1),
        name="far_back",
    )(k, v, docs, *args)


def permutation():
    p = lax.broadcasted_iota(jnp.int32, (T, T), 0)
    o = lax.broadcasted_iota(jnp.int32, (T, T), 1)
    return jnp.where(o == p % 32 * RES + bit_reversed(p // 32), 1.0, 0.0).astype(bf16)


def normalized(x):
    center = jnp.mean(x, axis=-1, keepdims=True)
    centered = x - center
    rstd = lax.rsqrt(jnp.mean(centered * centered, axis=-1, keepdims=True) + EPS)
    return centered * rstd, rstd


def norm_pullback(grad, xhat, rstd, gain):
    g = grad * gain
    gx = rstd * (g - jnp.mean(g, axis=-1, keepdims=True) - xhat * jnp.mean(g * xhat, axis=-1, keepdims=True))
    return gx, jnp.sum(grad * xhat, axis=0, keepdims=True), jnp.sum(grad, axis=0, keepdims=True)


def fetch(shards, buffer, sems, where_ref, rows):
    out = []
    for r, shard in enumerate(shards):
        at = pl.multiple_of(where_ref[r] * rows, rows)
        out.append(pltpu.make_async_copy(shard.at[pl.ds(0, rows)], buffer.at[pl.ds(at, rows)], sems.at[r]))
        out[-1].start()
    return out


def add_bias(values, row_ref, r):
    pick = jnp.where(lax.broadcasted_iota(jnp.int32, (16, values.shape[1]), 0) == r, 1.0, 0.0).astype(bf16)
    return values + tdot(row_ref, pick)


def block_lanes(g, level):
    at = g // (RES >> level) * (T >> level)
    return slice(at, at + (T >> level))


def head_slice(g):
    return slice(g * HD, (g + 1) * HD)


def project_kernel(levels, where_ref, w0, w1, w2, w3, vec_ref, bias_ref, docs_ref, x0_ref, x1_ref, *refs):
    q_ref, k_ref, v_ref, n_ref, in_ref, dout_ref = refs[:6]
    visit_refs = refs[6 : 5 + levels]
    w_ref, wt_ref, sems = refs[5 + levels :]
    copies = fetch((w0, w1, w2, w3), w_ref, sems, where_ref, D // 4)
    perm = permutation()
    gain, shift = vec_ref[0:1], vec_ref[2:3]

    def norm(x):
        xhat, _ = normalized(x.astype(f32))
        return ndot(perm, (xhat * gain + shift).astype(bf16)).astype(bf16)

    in_ref[...] = ndot(perm, x0_ref[...]).astype(bf16)
    n_ref[:T] = norm(x0_ref[...])
    n_ref[T:] = norm(x1_ref[:T])
    own_docs = bdot(jnp.broadcast_to(docs_ref[...].astype(f32), (8, T)).astype(bf16), perm)[0:1]
    near_docs = bdot(x1_ref[T:, :T], perm)[0:1]
    dout_ref[...] = jnp.concatenate([own_docs, near_docs], axis=1).astype(jnp.int32)
    for c in copies:
        c.wait()
    for part in range(3):
        wt = w_ref[:, part * D : (part + 1) * D].T
        for g in range(HEADS):
            h = int(ORDER[g])
            wt_ref[part * D + g * HD : part * D + (g + 1) * HD, :] = wt[head_slice(h)]
    n = n_ref[...]
    q_ref[...] = add_bias(bdot(wt_ref[:D, :], n_ref[:T]), bias_ref[...], 0).astype(bf16)
    for level in range(1, levels):
        width = T >> level
        visit = visit_refs[level - 1]
        for g in range(HEADS):
            visit[head_slice(g), :] = q_ref[head_slice(g), block_lanes(g, level)]
        rows = [own_docs[:, b * width : (b + 1) * width] for b in range(1 << level)]
        if level < 4:
            rows.append(jnp.zeros((16 - len(rows), width), f32))
        visit[D:, :] = jnp.concatenate(rows, axis=0).astype(bf16)
    k_ref[...] = bdot(wt_ref[D : 2 * D, :], n).astype(bf16)
    v_ref[...] = add_bias(bdot(wt_ref[2 * D :, :], n), bias_ref[...], 1).astype(bf16)


def project(levels, where, shards, vectors, biases, docs, tile, tile_near):
    return kernel_call(
        functools.partial(project_kernel, levels),
        in_specs=[SM] + [HB] * 4 + [VM] * 5,
        out_specs=[VM] * (5 + levels),
        out_shape=[shape_of(D, T), shape_of(D, 2 * T), shape_of(D, 2 * T), shape_of(2 * T, D), shape_of(T, D), shape_of(1, 2 * T, dtype=jnp.int32)]
        + [shape_of(D + 16, T >> level) for level in range(1, levels)],
        scratch_shapes=[pltpu.VMEM((D, 3 * D), bf16), pltpu.VMEM((3 * D, D), bf16), pltpu.SemaphoreType.DMA((4,))],
        cost_estimate=cost(1),
        name="project",
    )(where, *shards, vectors, biases, docs, tile, tile_near)


ERF_TOP = (0.00022905065861350646, 0.0034082910107109506, 0.050955695062380861, 0.18520832239976145, 1.128379143519084)
ERF_BOTTOM = (-1.1791602954361697e-7, 0.000023547966471313185, 0.0010179625278914885, 0.014070470171167667, 0.11098505178285362, 0.49746925110067538, 1.0)


def erf(x):
    x = jnp.clip(x, -3.7439211627767994, 3.7439211627767994)
    y = x * x
    top, bottom = ERF_TOP[0], ERF_BOTTOM[0]
    for c in ERF_TOP[1:]:
        top = top * y + c
    for c in ERF_BOTTOM[1:]:
        bottom = bottom * y + c
    return x * top / bottom


FF_PART = 768
FF_ROWS = 2 * FF_PART + D // 4


def merge_heads(o_ref, lm_ref, back, merged_ref, lmf_ref):
    for g in range(HEADS):
        base = lm_ref[g]
        parts, top = [], base
        blocks = [head_of(ref, g // FAR, BACK) for _, ref in back]
        for (level, _), block in zip(back, blocks):
            cols = block_lanes(g, level)
            rest = [jnp.full((1, n), -BIG, f32) for n in (cols.start, T - cols.stop)]
            parts.append(jnp.concatenate([x for x in (rest[0], number(block, g % FAR), rest[1]) if x.shape[1]], axis=1))
            top = jnp.maximum(top, parts[-1])
        weights = [jnp.exp2(x - top) for x in [base] + parts]
        total = sum(weights)
        scale = 1.0 / total
        out = o_ref[head_slice(g), :] * (weights[0] * scale)
        for (level, _), block, w in zip(back, blocks, weights[1:]):
            cols = block_lanes(g, level)
            add = head_of(block, g % FAR).astype(f32) * (w * scale)[:, cols]
            rest = [jnp.zeros((HD, n), f32) for n in (cols.start, T - cols.stop)]
            out = out + jnp.concatenate([x for x in (rest[0], add, rest[1]) if x.shape[1]], axis=1)
        merged_ref[head_slice(int(ORDER[g])), :] = out
        lmf_ref[g] = top + jnp.log2(total)


def middle_kernel(levels, back_levels, where_ref, *refs):
    shards, refs = refs[:4], refs[4:]
    o_ref, lm_ref, in_ref, cot_ref, vec_ref, hb_ref = refs[:6]
    n = len(back_levels)
    back = list(zip(back_levels, refs[6 : 6 + n]))
    refs = refs[6 + n :]
    enc_ref, mine_out, theirs_out, gm_ref, dd_ref, lmf_ref, gmid_ref, small_ref, gbias_ref = refs[:9]
    grad_out = lambda r, at, rows: (mine_out, theirs_out)[r % 2].at[r // 2, pl.ds(at, rows)]
    visit_refs, refs = refs[9 : 8 + levels], refs[8 + levels :]
    wo_ref, wu_ref, wd_ref, gd_ref, gu_ref, act_ref, merged_ref, y_ref, gn_ref, gy_ref, n2_ref, sems, osems = refs
    out_copies = fetch(shards, wo_ref, sems.at[0], where_ref, D // 4)
    up_copies, down_copies = [], []
    for r, shard in enumerate(shards):
        rows = pl.ds(pl.multiple_of(where_ref[r] * (D // 4), D // 4), D // 4)
        for c in range(4):
            dst = wu_ref.at[rows, pl.ds(c * FF_PART, FF_PART)]
            up_copies.append(pltpu.make_async_copy(shard.at[pl.ds((1 + c) * (D // 4), D // 4)], dst, sems.at[1 + c, r]))
            up_copies[-1].start()
    for r, shard in enumerate(shards):
        down_copies.append(pltpu.make_async_copy(shard.at[pl.ds(5 * (D // 4), FF_PART)], wd_ref.at[r], sems.at[5, r]))
        down_copies[-1].start()
    perm = permutation()
    gy_ref[...] = ndot(perm, cot_ref[...]).astype(bf16)
    merge_heads(o_ref, lm_ref, back, merged_ref, lmf_ref)
    merged = merged_ref[...].astype(bf16)
    for c in out_copies:
        c.wait()
    middle = in_ref[...].astype(f32) + tdot(merged, wo_ref[...]) + vec_ref[5:6]
    xhat, rstd = normalized(middle)
    n2_ref[...] = (xhat * vec_ref[1:2] + vec_ref[6:7]).astype(bf16)
    y_ref[...] = middle + vec_ref[7:8]
    gn_ref[...] = jnp.zeros_like(gn_ref)
    for c in up_copies:
        c.wait()
    down_parts = []
    for r in range(4):
        at = pl.multiple_of(where_ref[r] * FF_PART, FF_PART)
        cols = pl.ds(at, FF_PART)
        down_copies[r].wait()
        n2, gy = n2_ref[...], gy_ref[...]
        hidden = ndot(n2, wu_ref[:, cols]) + hb_ref[:, cols]
        phi = 0.5 + 0.5 * erf(hidden * 0.5**0.5)
        slope = phi + hidden * (jnp.exp(hidden * hidden * -0.5) * (2 * math.pi) ** -0.5)
        active = (hidden * phi).astype(bf16)
        y_ref[...] += ndot(active, wd_ref[r])
        gd_ref[r] = tdot(active, gy).astype(bf16)
        down_parts.append(pltpu.make_async_copy(gd_ref.at[r], grad_out(r, 0, FF_PART), osems.at[r]))
        down_parts[-1].start()
        gh = (slope * bdot(gy, wd_ref[r])).astype(bf16)
        gbias_ref[:, cols] = jnp.sum(gh.astype(f32), axis=0, keepdims=True)
        gu_ref[:, cols] = tdot(n2, gh).astype(bf16)
        gn_ref[...] += bdot(gh, wu_ref[:, cols])
    up_parts = []
    for r in range(4):
        at = pl.multiple_of(where_ref[r] * (D // 4), D // 4)
        for c in range(4):
            src = gu_ref.at[pl.ds(at, D // 4), pl.ds(c * FF_PART, FF_PART)]
            up_parts.append(pltpu.make_async_copy(src, grad_out(r, FF_PART + (1 + c) * (D // 4), D // 4), osems.at[8 + 4 * r + c]))
            up_parts[-1].start()
    enc_ref[...] = tdot(perm, y_ref[...].astype(bf16)).astype(bf16)
    gy = gy_ref[...].astype(f32)
    middle = in_ref[...].astype(f32) + tdot(merged, wo_ref[...]) + vec_ref[5:6]
    xhat, rstd = normalized(middle)
    gx, ggain, gshift = norm_pullback(gn_ref[...], xhat, rstd, vec_ref[1:2])
    gmid = gy + gx
    gmid_ref[...] = gmid
    gatt = gmid.astype(bf16)
    act_ref[...] = ndot(merged, gatt).astype(bf16)
    for r in range(4):
        at = pl.multiple_of(where_ref[r] * (D // 4), D // 4)
        down_parts.append(pltpu.make_async_copy(act_ref.at[pl.ds(at, D // 4)], grad_out(r, FF_PART, D // 4), osems.at[4 + r]))
        down_parts[-1].start()
    gm = bdot(wo_ref[...], gatt)
    prod = gm * merged_ref[...]
    gm = gm.astype(bf16)
    dds = [None] * HEADS
    for g in range(HEADS):
        h = head_slice(int(ORDER[g]))
        gm_ref[head_slice(g), :] = gm[h]
        dds[g] = jnp.sum(prod[h], axis=0, keepdims=True)
        dd_ref[g] = dds[g]
    for level in range(1, levels):
        for first in range(0, HEADS, FAR):
            features, numbers = [], []
            for g in range(first, first + FAR):
                cols = block_lanes(g, level)
                features.append(gm[head_slice(int(ORDER[g])), cols])
                numbers += [lmf_ref[g][:, cols], dds[g][:, cols]]
            at = first // FAR * OUT
            visit_refs[level - 1][at : at + OUT, :] = parcel(features, numbers, OUT)
    zero = jnp.zeros((4, D), f32)
    small_ref[...] = jnp.concatenate(
        [ggain, jnp.sum(gatt.astype(f32), axis=0, keepdims=True), gshift, jnp.sum(gy, axis=0, keepdims=True), zero], axis=0)
    for c in down_parts + up_parts:
        c.wait()


def middle(levels, where, shards, o, lm, back, inputs, cotangent, vectors, bias, after):
    s = shape_of
    ff = bias.shape[1]
    visits = [s(OUT * HEADS // FAR, T >> level) for level in range(1, levels)]
    return kernel_call(
        functools.partial(middle_kernel, levels, [b[0] for b in back]),
        after=after,
        in_specs=[SM] + [HB] * 4 + [VM] * (6 + len(back)),
        out_specs=[VM] + [HB] * 2 + [VM] * (6 + len(visits)),
        out_shape=[
            s(T, D), s(2, FF_ROWS, D), s(2, FF_ROWS, D),
            s(D, T), s(HEADS, 1, T, dtype=f32), s(HEADS, 1, T, dtype=f32), s(T, D, dtype=f32), s(8, D, dtype=f32), s(1, ff, dtype=f32),
        ] + visits,
        scratch_shapes=[
            pltpu.VMEM((D, D), bf16), pltpu.VMEM((D, ff), bf16), pltpu.VMEM((4, FF_PART, D), bf16),
            pltpu.VMEM((4, FF_PART, D), bf16), pltpu.VMEM((D, ff), bf16), pltpu.VMEM((D, D), bf16), pltpu.VMEM((D, T), f32),
            pltpu.VMEM((T, D), f32), pltpu.VMEM((T, D), f32), pltpu.VMEM((T, D), bf16), pltpu.VMEM((T, D), bf16),
            pltpu.SemaphoreType.DMA((6, 4)), pltpu.SemaphoreType.DMA((24,)),
        ],
        cost_estimate=cost(1),
        name="middle",
    )(where, *shards, o, lm, inputs, cotangent, vectors, bias, *[b[1] for b in back])


def natural(refs):
    rows = []
    for h in range(HEADS):
        g = head_slice(int(ORDER[h]))
        rows.append(sum(ref[g, :].astype(f32) for ref in refs).astype(bf16))
    return jnp.concatenate(rows, axis=0)


def to_blocks(where_ref, src_ref, out_refs, parts):
    rows = D // 4
    for r in range(4):
        at = pl.multiple_of(where_ref[r] * rows, rows)
        for part in range(parts):
            out_refs[r % 2][r // 2, part * rows : (part + 1) * rows, :] = src_ref[pl.ds(at, rows), part * D : (part + 1) * D]


def keys_kernel(where_ref, w0, w1, w2, w3, nk_ref, nv_ref, fk_ref, fv_ref, n_ref, vec_ref,
                send_ref, own_ref, mine_ref, theirs_ref, sums_ref, w_ref, gp_ref, gw_ref, sems):
    copies = fetch((w0, w1, w2, w3), w_ref, sems, where_ref, D // 4)
    gp_ref[:D] = natural((nk_ref, fk_ref))
    gp_ref[D:] = natural((nv_ref, fv_ref))
    for c in copies:
        c.wait()
    send = xdot(gp_ref[:, T:], w_ref[:, D:])
    send_ref[...] = send.astype(bf16)
    gw_ref[...] = xdot(n_ref[...], gp_ref[...]).astype(bf16)
    to_blocks(where_ref, gw_ref, (mine_ref, theirs_ref), 2)
    own_ref[...] = xdot(gp_ref[:, :T], w_ref[:, D:])
    xhat = (n_ref[T:].astype(f32) - vec_ref[2:3]) / vec_ref[0:1]
    rows = [bdot(jnp.ones((16, 2 * T), bf16), gp_ref[D:, :])[0:1]]
    rows += [jnp.sum(send * xhat, axis=0, keepdims=True), jnp.sum(send, axis=0, keepdims=True), jnp.zeros((5, D), f32)]
    sums_ref[...] = jnp.concatenate(rows, axis=0)


def keys_last(where, shards, grads, normed, vectors, after):
    s = shape_of
    return kernel_call(
        keys_kernel,
        after=after,
        in_specs=[SM] + [HB] * 4 + [VM] * 6,
        out_specs=[VM] * 5,
        out_shape=[s(T, D), s(T, D, dtype=f32), s(2, D // 2, D), s(2, D // 2, D), s(8, D, dtype=f32)],
        scratch_shapes=[pltpu.VMEM((D, 3 * D), bf16), pltpu.VMEM((2 * D, 2 * T), bf16), pltpu.VMEM((D, 2 * D), bf16), pltpu.SemaphoreType.DMA((4,))],
        cost_estimate=cost(1),
        name="keys_last",
    )(where, *shards, *grads, normed, vectors)


LAST_ROWS = 256


def queries_kernel(back_levels, where_ref, w0, w1, w2, w3, gq_ref, *refs):
    back = list(zip(back_levels, refs))
    n_ref, in_ref, vec_ref, small_ref, gbias_ref, own_ref, sums_ref = refs[len(back) : len(back) + 7]
    grad_ref, mine_ref, theirs_ref, w_ref, gp_ref, gw_ref, sems = refs[len(back) + 7 :]
    copies = fetch((w0, w1, w2, w3), w_ref, sems, where_ref, D // 4)
    for g in range(HEADS):
        rows = head_slice(g)
        total = gq_ref[rows, :].astype(f32)
        for level, ref in back:
            cols = block_lanes(g, level)
            rest = [jnp.zeros((HD, n), f32) for n in (cols.start, T - cols.stop)]
            total = total + jnp.concatenate([x for x in (rest[0], ref[rows, :].astype(f32), rest[1]) if x.shape[1]], axis=1)
        gp_ref[head_slice(int(ORDER[g])), :] = total.astype(bf16)
    gw_ref[...] = xdot(n_ref[:T], gp_ref[...]).astype(bf16)
    to_blocks(where_ref, gw_ref, (mine_ref, theirs_ref), 1)
    sums = bdot(jnp.ones((16, T), bf16), gp_ref[...])
    xhat, _ = normalized(in_ref[...].astype(f32))
    for c in copies:
        c.wait()
    grad = xdot(gp_ref[...], w_ref[:, :D]) + own_ref[...]
    grad_ref[...] = grad
    ggain = jnp.sum(grad * xhat, axis=0, keepdims=True) + sums_ref[1:2]
    gshift = jnp.sum(grad, axis=0, keepdims=True) + sums_ref[2:3]
    rows = [ggain, small_ref[0:1], gshift, sums[0:1], sums_ref[0:1], small_ref[1:4]]
    rows += [gbias_ref[:, i * D : (i + 1) * D] for i in range(4)]
    rows += [jnp.zeros((4, D), f32)]
    small = jnp.concatenate(rows, axis=0).astype(bf16)
    for out in (mine_ref, theirs_ref):
        for r in range(2):
            out[r, D // 4 : D // 4 + 16, :] = small
            out[r, D // 4 + 16 :, :] = jnp.zeros((LAST_ROWS - D // 4 - 16, D), bf16)


def queries_last(where, shards, gq, back, normed, inputs, vectors, small, gbias, own, sums, after):
    return kernel_call(
        functools.partial(queries_kernel, [b[0] for b in back]),
        after=after,
        in_specs=[SM] + [HB] * 4 + [VM] * (8 + len(back)),
        out_specs=[VM] * 3,
        out_shape=[shape_of(T, D, dtype=f32), shape_of(2, LAST_ROWS, D), shape_of(2, LAST_ROWS, D)],
        scratch_shapes=[pltpu.VMEM((D, 3 * D), bf16), pltpu.VMEM((D, T), bf16), pltpu.VMEM((D, D), bf16), pltpu.SemaphoreType.DMA((4,))],
        cost_estimate=cost(1),
        name="queries_last",
    )(where, *shards, gq, *[b[1] for b in back], normed, inputs, vectors, small, gbias, own, sums)


def last_kernel(grad_ref, in_ref, gmid_ref, vec_ref, got_ref, gt_ref):
    xhat, rstd = normalized(in_ref[...].astype(f32))
    gx, _, _ = norm_pullback(grad_ref[...] + got_ref[...].astype(f32), xhat, rstd, vec_ref[0:1])
    gt_ref[...] = tdot(permutation(), (gmid_ref[...] + gx).astype(bf16)).astype(bf16)


def last(grad, inputs, gmid, vectors, got, after):
    return kernel_call(
        last_kernel,
        after=after,
        in_specs=[VM] * 5,
        out_specs=VM,
        out_shape=shape_of(T, D),
        cost_estimate=cost(1),
        name="last",
    )(grad, inputs, gmid, vectors, got)


def gate_kernel(*refs):
    refs[-1][...] = jnp.zeros_like(refs[-1])


def gate(arrays, us):
    return kernel_call(
        gate_kernel,
        in_specs=[HB] * len(arrays),
        out_specs=VM,
        out_shape=shape_of(8, 128, dtype=f32),
        cost_estimate=cost(us),
        name="gate",
    )(*arrays)


def exchanged(x, axis, mask):
    return lax.ppermute(x, axis, [(i, i ^ mask) for i in range(lax.axis_size(axis))])


def added(a, b):
    return (a.astype(f32) + b.astype(f32)).astype(bf16)


def behind(x, other):
    return lax.optimization_barrier((x, other))[0]


class Chain:
    def __init__(self, line, steps):
        self.line, self.steps = line, list(steps)

    def begin(self, value, theirs=None):
        self.value = value
        self.launch(theirs)
        return self

    def launch(self, theirs=None):
        x, line = self.value, self.line
        if not self.steps:
            return
        step = self.steps[0]
        if step == "c":
            self.kept, self.got = x, exchanged(theirs, "fsdp", 1)
        elif step == "x":
            self.kept, self.got = x[:1], exchanged(x[1:], "fsdp", 2)
        elif step == "a":
            self.got = lax.all_to_all(x.reshape(line.seq, -1, D), "seq", 0, 0)
        elif step == "g":
            self.got = lax.all_to_all(jnp.broadcast_to(x, (line.seq,) + x.shape[1:]), "seq", 0, 0)
        elif step in ("F0", "F1", "F2"):
            self.kept, self.got = x, exchanged(x, "seq", 1 << int(step[1]))
        elif isinstance(step, int):
            half = x.shape[1] // 2
            mine = line.rank >> step & 1
            self.kept = lax.dynamic_slice_in_dim(x, mine * half, half, 1)
            self.got = exchanged(lax.dynamic_slice_in_dim(x, (1 - mine) * half, half, 1), "seq", 1 << step)
        else:
            self.got = exchanged(x, "seq", 1 << int(step))

    def advance(self):
        step, got = self.steps.pop(0), behind(self.got, self.line.token)
        if step == "a":
            out = jnp.sum(got.astype(f32), axis=0, keepdims=True).astype(bf16)
        elif step == "g":
            out = got.reshape(1, -1, D)
        elif isinstance(step, str) and step.isdigit():
            x, low = self.value, (self.line.rank >> int(step) & 1) == 0
            out = jnp.concatenate([jnp.where(low, x, got), jnp.where(low, got, x)], axis=1)
        else:
            out = added(self.kept, got)
            if step == "x":
                for bit in range(3, self.line.seq.bit_length() - 1):
                    if "a" not in self.steps:
                        out = added(out, exchanged(out, "seq", 1 << bit))
        self.value = self.line.token = out
        self.launch()


class Line:
    def __init__(self, rank, seq, token):
        self.rank, self.seq, self.token = rank, seq, token


def local(tiles, documents, cotangent, w_qkv, w_out, w_up, w_down, gains, shifts, hidden_bias):
    seq = lax.axis_size("seq")
    rank = lax.axis_index("seq")
    part = lax.axis_index("fsdp")
    levels = min(BRANCHES, (seq * T // SEG_BASE).bit_length())
    where = jnp.stack([part ^ r for r in range(4)]).astype(jnp.int32)
    visits = [(level, (1 << level) + 2 * c) for level in range(1, levels) for c in range(1 << level - 1)]
    cols = gains.shape[1]

    packed = jnp.concatenate([gains, shifts, hidden_bias.reshape(-1, cols)], axis=0).reshape(1, -1)
    w_ext = jnp.concatenate([w_qkv, jnp.pad(packed, ((0, 7), (0, 0)))], axis=0)
    qkv_far = exchanged(w_ext, "fsdp", 2)
    tile = tiles[0]
    docs_row = jnp.pad(documents.astype(bf16), ((0, 7), (0, D - T)))
    tile_near = exchanged(jnp.concatenate([tile, docs_row], axis=0), "seq", 1)
    stacked_up = w_up.reshape(cols, -1, D).swapaxes(0, 1).reshape(-1, D)
    w_ff = jnp.concatenate([w_out, stacked_up, w_down], axis=0)
    ff_far = exchanged(w_ff, "fsdp", 2)
    qkv_near = exchanged(w_ext, "fsdp", 1)
    qkv_shards = (w_ext, qkv_near, qkv_far, exchanged(behind(qkv_far, tile_near), "fsdp", 1))
    ff_near = exchanged(w_ff, "fsdp", 1)

    stacked = jnp.stack([w[cols].reshape(-1, cols) for w in qkv_shards])
    in_order = jnp.stack([lax.dynamic_index_in_dim(stacked, part ^ s, 0, keepdims=False) for s in range(4)])
    rows = in_order[:, :8].transpose(1, 0, 2).reshape(8, D)
    vectors = rows.astype(f32)
    bias_row = in_order[:, 8:].reshape(1, -1).astype(f32)
    by_head = rows[3:5].reshape(2, 2, 2, 2, 2, HD).transpose(0, 4, 3, 2, 1, 5).reshape(2, D)
    biases = jnp.concatenate([by_head, jnp.zeros((14, D), bf16)], axis=0)

    q, k, v, normed, inputs, docs, *queries = project(levels, where, qkv_shards, vectors, biases, documents, tile, tile_near)
    guests = [(level, exchanged(queries[level - 1], "seq", mask)) for level, mask in visits]
    o, lm = attend_near(q, k, v, docs)
    partial = attend_far(k, v, docs, guests, [lm])
    back = [(level, exchanged(x, "seq", mask)) for (level, mask), x in zip(visits, partial)]
    shards = (w_ff, ff_near, ff_far, exchanged(behind(ff_far, [x for _, x in back]), "fsdp", 1))

    encoded, early_mine, early_theirs, gmerged, dd, lmf, gmid, small, gbias, *send = middle(
        levels, where, shards, o, lm, back, inputs, cotangent[0], vectors, bias_row, [])
    early_theirs = exchanged(early_theirs, "fsdp", 1)
    guests = [guest + (exchanged(send[level - 1], "seq", mask),) for guest, (level, mask) in zip(guests, visits)]
    nears = near_back(q, k, v, docs, gmerged, lmf, dd, 0, 4)
    early = added(early_mine, behind(early_theirs, nears[0]))
    n = FF_PART + D // 4
    line = Line(rank, seq, early)
    up = Chain(line, ["x", 1, 0, 2, "2", "0", "1"]).begin(early[:, n:])
    down = Chain(line, [0, "x", 1, 2, "2", "1", "0"]).begin(early[:, :n])
    keys = Chain(line, ["c", "x", 0, 1, 2, "2", "1", "0"])
    late = Chain(line, ["c", "x", "a", "g"])
    gq, gk, gv = near_back(q, k, v, docs, gmerged, lmf, dd, 4, 12, nears, [early])
    far_k, far_v, *turned = far_back(k, v, docs, guests, [gq])
    back = [(level, exchanged(x, "seq", mask)) for (level, mask), x in zip(visits, turned)]

    returned = gate([x for _, x in back], 30)

    line.token = far_k
    up.advance()
    down.advance()
    to_near, own_part, keys_mine, keys_theirs, sums = keys_last(
        where, qkv_shards, (gk, gv, far_k, far_v), normed, vectors, [line.token])
    got = exchanged(to_near, "seq", 1)
    keys.begin(keys_mine, keys_theirs)
    grad, late_mine, late_theirs = queries_last(
        where, qkv_shards, gq, back, normed, inputs, vectors, small, gbias, own_part, sums, [returned])
    late.begin(late_mine, late_theirs)
    line.token = late_mine
    for chain in (up, keys, down, late, up, late, keys, down, up, keys, down, late, up, None, keys, down, up, keys, down, keys, up, keys, late, down, keys):
        if chain is None:
            grad_tiles = line.token = last(grad, inputs, gmid, vectors, got, [line.token])
        else:
            chain.advance()
    sum_up, sum_down, late_keys, late = [c.value[0].astype(f32) for c in (up, down, keys, late)]

    side_by_side = lambda a: a.reshape(-1, D // 4, D).swapaxes(0, 1).reshape(D // 4, -1)
    tiny = late[D // 4 : D // 4 + 16]
    mine = lax.dynamic_slice_in_dim(tiny[:8], part * cols, cols, 1)
    sum_bias = lax.dynamic_slice_in_dim(tiny[8:12], part, 1, 0).reshape(-1)
    return (
        encoded[None],
        grad_tiles[None],
        side_by_side(jnp.concatenate([late[: D // 4], late_keys], axis=0)), sum_down[FF_PART:], side_by_side(sum_up), sum_down[:FF_PART],
        mine[:2], mine[2:], sum_bias,
    )


def solution(mesh):
    tokens, rows, cols = P("fsdp", "seq", None), P("fsdp", None), P(None, "fsdp")
    return jax.shard_map(
        local,
        mesh=mesh,
        in_specs=(tokens, P("fsdp", "seq"), tokens, rows, rows, rows, rows, cols, cols, P("fsdp")),
        out_specs=(tokens, tokens, rows, rows, rows, rows, cols, cols, P("fsdp")),
        check_vma=False,
    )
```
